128 devices in a mesh: fsdp: 4 (over x_hi, core), ctx: 32 (over y, x_lo, z).
Axes of the slice: x: 4 (x_hi: 2, x_lo: 2; x = x_hi * 2 + x_lo), y: 4, z: 4, core: 2. Of those that a mesh axis runs over, the one named last changes fastest.
Arguments:
- tokens: bfloat16 [4, 4096, 1088], P('fsdp', 'ctx'), may hold values from -6 to 6
- cotangent: bfloat16 [4, 4096, 1088], P('fsdp', 'ctx'), may hold values from -6 to 6
- lengths: int32 [4], P('fsdp'), may hold values from 2049 to 4096, as said below
- block_order: int32 [32], replicated, may hold values from 0 to 31, each once
- ln1_gain: bfloat16 [1088], P('ctx'), may hold values from 0.5 to 1.5
- ln1_bias: bfloat16 [1088], P('ctx'), may hold values from -1.75 to 1.75
- w_qkv: bfloat16 [1088, 3264], P('ctx', 'fsdp'), may hold values from -0.1875 to 0.1875
- q_bias: bfloat16 [1088], P('ctx'), may hold values from -1.75 to 1.75
- v_bias: bfloat16 [1088], P('ctx'), may hold values from -1.75 to 1.75
- w_out: bfloat16 [1088, 1088], P('ctx', 'fsdp'), may hold values from -6 to 6
- out_bias: bfloat16 [1088], P('ctx'), may hold values from -1.75 to 1.75
- ln2_gain: bfloat16 [1088], P('ctx'), may hold values from 0.5 to 1.5
- ln2_bias: bfloat16 [1088], P('ctx'), may hold values from -1.75 to 1.75
- w_fc: bfloat16 [1088, 4352], P('ctx', 'fsdp'), may hold values from -0.1875 to 0.1875
- fc_bias: bfloat16 [4352], P('ctx'), may hold values from -1.75 to 1.75
- w_proj: bfloat16 [4352, 1088], P('ctx', 'fsdp'), may hold values from -0.09375 to 0.09375
- proj_bias: bfloat16 [1088], P('ctx'), may hold values from -1.75 to 1.75
Outputs:
- layer_out: bfloat16 [4, 4096, 1088], P('fsdp', 'ctx')
- grad_tokens: bfloat16 [4, 4096, 1088], P('fsdp', 'ctx')
- grad_ln1_gain: float32 [1088], P('ctx')
- grad_ln1_bias: float32 [1088], P('ctx')
- grad_w_qkv: float32 [1088, 3264], P('ctx', 'fsdp')
- grad_q_bias: float32 [1088], P('ctx')
- grad_v_bias: float32 [1088], P('ctx')
- grad_w_out: float32 [1088, 1088], P('ctx', 'fsdp')
- grad_out_bias: float32 [1088], P('ctx')
- grad_ln2_gain: float32 [1088], P('ctx')
- grad_ln2_bias: float32 [1088], P('ctx')
- grad_w_fc: float32 [1088, 4352], P('ctx', 'fsdp')
- grad_fc_bias: float32 [4352], P('ctx')
- grad_w_proj: float32 [4352, 1088], P('ctx', 'fsdp')
- grad_proj_bias: float32 [1088], P('ctx')
The draws below stay inside these ranges and needn't reach their ends.
Inputs may be any that keep to these rules, and one draw needn't show every extreme that they name: `lengths`: each slot holds one sequence starting at position 0 with this many valid tokens; at least one slot is entirely valid. Device c of ctx holds causal blocks block_order[c] and 2 * 32 - 1 - block_order[c], each of 64 positions, in that order.
All inputs are finite; a program needn't handle non-finite values.
Results may differ from the reference program's by a relative error of at most 0.04.
Values may be sent and summed in bfloat16 or wider, within the bound.
No kernel may reach another device: no remote copies, remote signals or barrier semaphores. Data moves between devices by JAX's collectives and lax.ppermute only.
A program may use at most 256 MiB of HBM per device.

```python
import math
import jax
import jax.numpy as jnp
from jax import lax

D = 1088
HEADS = 17
HEAD_DIM = 64
FF = 4352
BLK = 64
SLOTS = 4
SLOT = 4096
N_CTX = 32


def draw_lengths(key, part):
    key = jax.random.fold_in(key, 11)
    first_key, second_key = jax.random.split(key)
    drawn = jax.random.randint(first_key, (SLOTS,), SLOT // 2 + 1, SLOT + 1)
    chosen = jax.random.randint(second_key, (), 0, SLOTS)
    return jnp.where(jnp.arange(SLOTS) == chosen, SLOT, drawn).astype(jnp.int32)


def levels(rng, shape, shards, least, high):
    loudness = 1.0
    for position, shards_of in shards:
        heights = jax.random.uniform(jax.random.fold_in(jax.random.fold_in(rng, 6), position), (shards_of,), jnp.float32, least / len(shards), high / len(shards))
        loudness = loudness * jnp.repeat(jnp.exp(heights), shape[position] // shards_of).reshape((-1,) + (1,) * (len(shape) - 1 - position))
    return loudness


def gaussian(stream_key, extent, deviation, limit, shards=(), kind=jnp.bfloat16):
    entries = deviation * jax.random.normal(stream_key, extent, jnp.float32)
    if shards:
        entries = entries * levels(stream_key, extent, shards, -0.22, 0.18)
    return jnp.clip(entries, -limit, limit).astype(kind)


def setup_inputs(seed: int = 0) -> dict:
    key_list = jax.random.split(jax.random.key(seed), 18)
    return {
        "tokens": gaussian(key_list[0], (SLOTS, SLOT, D), 1.0, 6.0, ((0, 4), (1, 32))),
        "cotangent": gaussian(key_list[1], (SLOTS, SLOT, D), 1.0, 6.0, ((0, 4), (1, 32))),
        "lengths": draw_lengths(jax.random.fold_in(key_list[17], 71), 0),
        "block_order": jax.random.permutation(key_list[3], N_CTX).astype(jnp.int32),
        "ln1_gain": jnp.clip(1.0 + 0.1 * jax.random.normal(key_list[4], (D,), jnp.float32), 0.5, 1.5).astype(jnp.bfloat16),
        "ln1_bias": gaussian(key_list[5], (D,), 0.3, 1.75, ((0, 32),)),
        "w_qkv": gaussian(key_list[6], (D, 3 * D), D ** -0.5, 0.1875, ((0, 32), (1, 4))),
        "q_bias": gaussian(key_list[7], (D,), 0.3, 1.75, ((0, 32),)),
        "v_bias": gaussian(key_list[8], (D,), 0.3, 1.75, ((0, 32),)),
        "w_out": gaussian(key_list[9], (D, D), (0.7 * (SLOT // 2) ** 0.5 * D ** -0.5), 6.0, ((0, 32), (1, 4))),
        "out_bias": gaussian(key_list[10], (D,), 0.3, 1.75, ((0, 32),)),
        "ln2_gain": jnp.clip(1.0 + 0.1 * jax.random.normal(key_list[11], (D,), jnp.float32), 0.5, 1.5).astype(jnp.bfloat16),
        "ln2_bias": gaussian(key_list[12], (D,), 0.3, 1.75, ((0, 32),)),
        "w_fc": gaussian(key_list[13], (D, FF), D ** -0.5, 0.1875, ((0, 32), (1, 4))),
        "fc_bias": gaussian(key_list[14], (FF,), 0.3, 1.75, ((0, 32),)),
        "w_proj": gaussian(key_list[15], (FF, D), FF ** -0.5, 0.09375, ((0, 32), (1, 4))),
        "proj_bias": gaussian(key_list[16], (D,), 0.3, 1.75, ((0, 32),)),
    }


@jax.custom_vjp
def low(v):
    return lax.optimization_barrier(v.astype(jnp.bfloat16)).astype(jnp.float32)

@jax.custom_vjp
def low_back(v):
    return v

def low_keep(v):
    return (low(v), None)

def low_pass(kept, grad):
    return (grad,)

def back_keep(v):
    return (v, None)

def back_low(kept, grad):
    return (low(grad),)
low.defvjp(low_keep, low_pass)
low_back.defvjp(back_keep, back_low)

def highest_dot(left, right):
    return jnp.dot(left, right, precision=lax.Precision.HIGHEST, preferred_element_type=jnp.float32)

def normalize(values):
    center = values - lax.optimization_barrier(jnp.mean(values, axis=-1, keepdims=True))
    spread = lax.optimization_barrier(jnp.mean(center * center, axis=-1, keepdims=True))
    return center * lax.rsqrt(spread + 1e-05)

def token_positions(order_table):
    row_ids = jnp.arange(SLOT, dtype=jnp.int32)
    device_ids = row_ids // (2 * BLK)
    inner_ids = row_ids % (2 * BLK)
    pair_ids = order_table[device_ids].astype(jnp.int32)
    placed = jnp.where(inner_ids < BLK, pair_ids * BLK + inner_ids, (2 * N_CTX - 1 - pair_ids) * BLK + inner_ids - BLK)
    return placed.astype(jnp.int32)

def attend(queries, keys, values, positions, valid):
    block_size = math.gcd(SLOT, 512)
    query_blocks = queries.reshape(SLOT // block_size, block_size, HEADS, HEAD_DIM)
    key_heads = keys.reshape(SLOT, HEADS, HEAD_DIM)
    value_heads = values.reshape(SLOT, HEADS, HEAD_DIM)
    block_pos = positions.reshape(SLOT // block_size, block_size)
    attn_scale = HEAD_DIM ** (-0.5)

    def one_block(inputs):
        query_block, query_pos = inputs
        scores = jnp.einsum('qhd,khd->hqk', query_block, key_heads, precision=lax.Precision.HIGHEST)
        scaled = low_back(scores * attn_scale)
        allowed = valid[None, :] & (positions[None, :] <= query_pos[:, None])
        masked = jnp.where(allowed[None], scaled, -1e+30)
        row_peak = lax.optimization_barrier(jnp.max(masked, axis=-1, keepdims=True))
        expd = jnp.where(allowed[None], jnp.exp(masked - row_peak), 0.0)
        probs = low(expd / lax.optimization_barrier(jnp.sum(expd, axis=-1, keepdims=True)))
        mixed = jnp.einsum('hqk,khd->qhd', probs, value_heads, precision=lax.Precision.HIGHEST)
        return mixed.reshape(block_size, HEADS * HEAD_DIM)
    result = lax.map(jax.checkpoint(one_block), (query_blocks, block_pos))
    return result.reshape(SLOT, HEADS * HEAD_DIM)

def layer_forward(tokens_f, params, positions, valid):
    ln1_gain, ln1_bias, w_qkv, q_bias, v_bias, w_out, out_bias, ln2_gain, ln2_bias, w_fc, fc_bias, w_proj, proj_bias = params
    normed = low(normalize(tokens_f) * ln1_gain + ln1_bias)
    projected = highest_dot(normed, w_qkv)
    queries = low(low_back(projected[:, :D] + q_bias))
    keys = low(low_back(projected[:, D:2 * D]))
    values = low(low_back(projected[:, 2 * D:] + v_bias))
    attended = low(low_back(attend(queries, keys, values, positions, valid)))
    branch = low_back(highest_dot(attended, w_out) + out_bias)
    middle = tokens_f + branch
    second = low(normalize(middle) * ln2_gain + ln2_bias)
    hidden = low_back(highest_dot(second, w_fc) + fc_bias)
    active = low(jax.nn.gelu(hidden, approximate=True))
    final = highest_dot(active, w_proj) + proj_bias
    return valid[:, None].astype(jnp.float32) * (middle + final)

def reference(tokens, cotangent, lengths, block_order, ln1_gain, ln1_bias, w_qkv, q_bias, v_bias, w_out, out_bias, ln2_gain, ln2_bias, w_fc, fc_bias, w_proj, proj_bias):
    positions = token_positions(block_order)
    params = tuple((weight.astype(jnp.float32) for weight in (ln1_gain, ln1_bias, w_qkv, q_bias, v_bias, w_out, out_bias, ln2_gain, ln2_bias, w_fc, fc_bias, w_proj, proj_bias)))

    def one_slot(totals, inputs):
        slot_tokens, slot_cot, slot_length = inputs
        valid = positions < slot_length

        def forward(tokens_f, weights):
            return layer_forward(tokens_f, weights, positions, valid)
        result, pullback = jax.vjp(forward, slot_tokens.astype(jnp.float32), params)
        grad_in, grad_params = pullback(slot_cot.astype(jnp.float32))
        totals = jax.tree.map(lambda left, right: left + right, totals, grad_params)
        return (totals, (result.astype(jnp.bfloat16), grad_in.astype(jnp.bfloat16)))
    zeros_init = jax.tree.map(jnp.zeros_like, params)
    totals, (outputs, grad_inputs) = lax.scan(one_slot, zeros_init, (tokens, cotangent, lengths))
    return (outputs, grad_inputs, totals[0], totals[1], totals[2], totals[3], totals[4], totals[5], totals[6], totals[7], totals[8], totals[9], totals[10], totals[11], totals[12])
```

```python
import jax
import jax.numpy as jnp
import numpy as np
from jax import lax
from jax.sharding import Mesh
from jax.sharding import PartitionSpec as P

F32 = jnp.float32
BF16 = jnp.bfloat16
HD = 64
SCALE = HD**-0.5
NEG = -1e30
AXES = ("xh", "co", "y", "xl", "z")
CTX = ("y", "xl", "z")
YZ = ("y", "z")
X = ("xh", "xl")
SWAP = [(0, 1), (1, 0)]

PIECE = 72
ORDER = np.full((16, PIECE), -1, np.int32)
for _n in range(16):
    for _xl in range(2):
        _c = (_n // 4) * 8 + _xl * 4 + _n % 4
        ORDER[_n, _xl * 34 : _xl * 34 + 34] = _c * 34 + np.arange(34)
ORDER = ORDER.reshape(-1)
DP = 16 * PIECE


def ring(n, s):
    return [(i, (i + s) % n) for i in range(n)]


def swap(v):
    return lax.ppermute(v, "co", SWAP)


def nt(a, b):
    return lax.dot_general(a, b, (((1,), (1,)), ((), ())), preferred_element_type=F32)


def nn(a, b):
    return lax.dot_general(a, b, (((1,), (0,)), ((), ())), preferred_element_type=F32)


def tn(a, b):
    return lax.dot_general(a, b, (((0,), (0,)), ((), ())), preferred_element_type=F32)


def heads(v):
    return jnp.transpose(v.reshape(2, 64, 17, 64), (0, 2, 1, 3))


def every(v):
    return jnp.broadcast_to(v[:, 16:], (2, 16, 64, 64))


def pairs_of(*parts):
    rows = [jnp.concatenate(pair, axis=3) for pair in parts]
    return jnp.concatenate(rows, axis=2).reshape(32, 64 * len(parts), 128)


def merge(first, last):
    whole = jnp.concatenate([first, last[:, None]], axis=1)
    return jnp.transpose(whole, (0, 2, 1, 3)).reshape(128, 1088)


def take(v, i):
    return lax.dynamic_index_in_dim(v, i, 0, keepdims=False)


def tile_attend(q, k, v, limit, at):
    s = jnp.where(at[:, None] <= limit[None, :], nt(k, q) * SCALE, NEG)
    top = jnp.max(s, axis=0, keepdims=True)
    e = jnp.exp(s - top)
    total = jnp.sum(e, axis=0, keepdims=True)
    out = tn(v, e.astype(BF16)) / total
    return out, top + jnp.log(total)


def tile_back(q, k, v, limit, at, g, out, lse):
    s = jnp.where(at[:, None] <= limit[None, :], nt(k, q) * SCALE, NEG)
    e = jnp.exp(s - lse)
    delta = jnp.sum(g.astype(F32).T * out, axis=0, keepdims=True)
    ds = (e * (nt(v, g) - delta)).astype(BF16)
    return tn(ds, k) * SCALE, nn(ds, q) * SCALE, nn(e.astype(BF16), g)


def standardize(values):
    center = values - jnp.mean(values, axis=-1, keepdims=True)
    spread = jnp.mean(center * center, axis=-1, keepdims=True)
    inverse = lax.rsqrt(spread + 1e-05)
    return (center * inverse, inverse)


def norm_back(grad_result, hat, inverse, gain):
    scaled = grad_result * gain
    first = jnp.mean(scaled, axis=-1, keepdims=True)
    second = jnp.mean(scaled * hat, axis=-1, keepdims=True)
    grad_input = inverse * (scaled - first - hat * second)
    return (grad_input, jnp.sum(grad_result * hat, axis=0), jnp.sum(grad_result, axis=0))


def order_matrix():
    order = jnp.asarray(ORDER)
    return (jnp.arange(16 * 68)[:, None] == order[None, :]).astype(BF16)


def to_order(v):
    return nn(v, order_matrix()).astype(BF16)


def from_order(v):
    return nt(v, order_matrix())


def from_order_wide(v):
    high = lax.reduce_precision(v, 8, 7)
    return from_order(high.astype(BF16)) + from_order((v - high).astype(BF16))


def gather_ring(piece, axis, at):
    out = jnp.zeros((4,) + piece.shape, piece.dtype)
    out = lax.dynamic_update_index_in_dim(out, piece, at, 0)
    for s in (1, 3, 2):
        got = lax.ppermute(piece, axis, ring(4, s))
        out = lax.dynamic_update_index_in_dim(out, got, (at + 4 - s) % 4, 0)
    return out


def sum_ring(pieces, axis, at, dim=0):
    total = lax.dynamic_index_in_dim(pieces, at, dim, keepdims=False).astype(F32)
    for s in (1, 3, 2):
        part = lax.dynamic_index_in_dim(pieces, (at + s) % 4, dim, keepdims=False)
        total = total + lax.ppermute(part, axis, ring(4, s)).astype(F32)
    return total


def rows_of_x(four):
    top = jnp.concatenate([four[0], four[2]], axis=1)
    low = jnp.concatenate([four[1], four[3]], axis=1)
    return jnp.concatenate([top, low, jnp.zeros((4, top.shape[1]), top.dtype)], axis=0)


def x_of_rows(rows):
    n = rows.shape[1] // 2
    return jnp.stack([rows[:34, :n], rows[34:68, :n], rows[:34, n:], rows[34:68, n:]])


def body(
    tokens,
    cotangent,
    lengths,
    block_order,
    ln1_gain,
    ln1_bias,
    w_qkv,
    q_bias,
    v_bias,
    w_out,
    out_bias,
    ln2_gain,
    ln2_bias,
    w_fc,
    fc_bias,
    w_proj,
    proj_bias,
):
    d = 1088
    xh, co, y, xl, z = (lax.axis_index(a) for a in AXES)
    ctx = y * 8 + xl * 4 + z
    x = xh * 2 + xl
    even = co == 0

    def both(own, other):
        return jnp.where(even, own, other), jnp.where(even, other, own)

    qkv_piece = rows_of_x(gather_ring(w_qkv, X, x))
    qkv_a = gather_ring(qkv_piece[:, :816], "z", z).reshape(4 * PIECE, 816)
    qkv_b = gather_ring(qkv_piece[:, 816:], "y", y)
    qkv_a = gather_ring(qkv_a, "y", y).reshape(DP, 816)
    qkv_b = gather_ring(qkv_b, "z", z)
    qkv_b = jnp.swapaxes(qkv_b, 0, 1).reshape(DP, 816)
    fc_keep, fc_half = both(w_fc[:, :544], w_fc[:, 544:])
    fc_own = jnp.concatenate(both(fc_keep, swap(fc_half)), axis=1)
    proj_own = lax.ppermute(w_proj, ("co", "xl"), [(0, 0), (1, 2), (2, 1), (3, 3)])
    four = gather_ring(jnp.concatenate([w_out, fc_own], axis=1), X, x)
    fc_piece = jnp.concatenate([rows_of_x(four[:, :, 272:]), rows_of_x(four[:, :, :272])], axis=1)
    four = gather_ring(proj_own, X, x)
    proj_piece = jnp.concatenate([four[0], four[1], four[2], four[3]], axis=1)
    fc_out = lax.all_gather(fc_piece, YZ, axis=0, tiled=True)
    proj = lax.all_gather(proj_piece, YZ, axis=0, tiled=True)
    fc = fc_out[:, :2176]
    out_w = fc_out[:, 2176:]

    vectors = jnp.concatenate(
        [ln1_gain, ln1_bias, q_bias, v_bias, out_bias, ln2_gain, ln2_bias, proj_bias, fc_bias]
    ).astype(F32)
    vectors = lax.all_to_all(
        jnp.broadcast_to(vectors[None], (32, 408)), CTX, split_axis=0, concat_axis=0, tiled=True
    )
    gain_one, bias_one, query_bias, value_bias, branch_bias, gain_two, bias_two, final_bias = (
        vectors[:, 34 * i : 34 * i + 34].reshape(1, d) for i in range(8)
    )
    hidden_bias = vectors[:, 272:].reshape(4, 2, 544)
    hidden_bias = jnp.where(even, hidden_bias[:, 0], hidden_bias[:, 1]).reshape(1, 2176)

    pair = lax.dynamic_index_in_dim(block_order, ctx, 0, keepdims=False)
    keep = (co + pair) % 2
    sent = jnp.concatenate([tokens, cotangent], axis=0)
    low = keep == 0
    kept = jnp.where(low, sent[:, :64], sent[:, 64:])
    sent = jnp.where(low, sent[:, 64:], sent[:, :64])
    slots = jnp.stack(both(kept, swap(sent)), axis=1).reshape(2, 128, d)
    length = jnp.concatenate(both(lengths, swap(lengths)))
    block = jnp.where(keep == 0, pair, 63 - pair)
    at = block * 64 + jnp.arange(64, dtype=jnp.int32)
    valid = (at[None, :] < length[:, None]).reshape(128, 1)
    mask = valid.astype(F32)

    blocks = 2 * jnp.arange(32, dtype=jnp.int32)[None, :] + jnp.arange(2, dtype=jnp.int32)[:, None]
    pairs = jnp.where(blocks < 32, blocks, 63 - blocks)
    match = pairs[:, :, None] == block_order[None, None, :]
    found = jnp.sum(jnp.where(match, jnp.arange(32, dtype=jnp.int32), 0), axis=2).astype(jnp.int32)
    own = jnp.where(even, found[0], found[1])
    oth = jnp.where(even, found[1], found[0])
    index = (block - co) // 2
    info = jnp.stack(
        [co, ctx % 16, jnp.where(index < 16, index, 31 - index), jnp.where(ctx < 16, length[0], length[1])]
    ).astype(jnp.int32)

    tokens_f = slots[0].astype(F32)
    first_hat, first_inverse = standardize(tokens_f)
    normed = to_order((first_hat * gain_one + bias_one).astype(BF16))
    normed = jnp.concatenate([normed, swap(normed)], axis=0)
    bias = jnp.concatenate([query_bias, jnp.zeros((1, d), F32), value_bias], axis=1)
    bias_a = jnp.where(even, bias[:, :816], bias[:, 816:1632])
    bias_b = jnp.where(even, bias[:, 1632:2448], bias[:, 2448:])
    part_a = (nn(normed, qkv_a) + bias_a).astype(BF16)
    part_b = (nn(normed, qkv_b) + bias_b).astype(BF16)
    f0, f1 = both(part_a[:128], swap(part_a[128:]))
    f2, f3 = both(part_b[:128], swap(part_b[128:]))
    whole = jnp.concatenate([f0, f1, f2, f3], axis=1)
    q, k, v = (heads(whole[:, i * d : i * d + d]) for i in range(3))
    first, last = slice(0, 16), slice(16, 17)
    sent = pairs_of((q[:, first], every(q)), (k[:, first], v[:, first]), (every(v), every(k)))
    xs = lax.all_to_all(sent, CTX, split_axis=0, concat_axis=0, tiled=True)
    xo = swap(xs[:, 64:])
    turn = info[1]
    xs, xo = xs[own], xo[oth]
    inner = jnp.arange(64, dtype=jnp.int32)
    at_q = ((2 * jnp.arange(32, dtype=jnp.int32) + co)[:, None] * 64 + inner).reshape(2048)
    at_o = ((2 * jnp.arange(32, dtype=jnp.int32) + 1 - co)[:, None] * 64 + inner).reshape(2048)
    q_all = xs[:, :64, :64].reshape(2048, 64)
    pair_q = jnp.concatenate([take(xs, turn)[:64, 64:], take(xs, 31 - turn)[:64, 64:]], axis=0)
    k_own, v_own = xs[:, 64:128, :64].reshape(2048, 64), xs[:, 64:128, 64:].reshape(2048, 64)
    k_oth, v_oth = xo[:, :64, :64].reshape(2048, 64), xo[:, :64, 64:].reshape(2048, 64)
    v_16 = jnp.concatenate([xs[:, 128:, :64].reshape(2048, 64), xo[:, 64:, :64].reshape(2048, 64)], axis=0)
    k_16 = jnp.concatenate([xs[:, 128:, 64:].reshape(2048, 64), xo[:, 64:, 64:].reshape(2048, 64)], axis=0)
    bound = info[3] - 1
    at_all = jnp.concatenate([at_q, at_o])
    at_pair = jnp.concatenate([take(at_q.reshape(32, 64), turn), take(at_q.reshape(32, 64), 31 - turn)])
    tiles = []
    for j in range(4):
        r, n = slice(512 * j, 512 * j + 512), slice(0, 512 * j + 512)
        keys = jnp.concatenate([k_own[n], k_oth[n]], axis=0)
        values = jnp.concatenate([v_own[n], v_oth[n]], axis=0)
        at = jnp.concatenate([at_q[n], at_o[n]])
        limit = jnp.minimum(at_q[r], bound)
        tiles.append((r, n, keys, values, limit, at, q_all[r]))
    outs = [tile_attend(q, keys, values, limit, at) for r, n, keys, values, limit, at, q in tiles]
    pair_limit = jnp.minimum(at_pair, bound)
    out_16, lse_16 = tile_attend(pair_q, k_16, v_16, pair_limit, at_all)
    inverse = jnp.sum(jnp.where(own[None, :] == jnp.arange(32)[:, None], jnp.arange(32), 0), axis=1)
    is_turn = jnp.arange(32)[:, None, None]
    low_16 = out_16.T.reshape(2, 64, 64)
    wide = jnp.where(is_turn == turn, low_16[0], jnp.where(is_turn == 31 - turn, low_16[1], 0.0))
    low_all = jnp.concatenate([o.T for o, _ in outs], axis=0).reshape(32, 64, 64)
    o_sent = jnp.concatenate([wide, low_all], axis=2).astype(BF16)[inverse]
    o_got = lax.all_to_all(o_sent, CTX, split_axis=0, concat_axis=0, tiled=True)
    o_got = o_got.reshape(2, 16, 64, 128)
    home_turn = info[2]

    def turned(v):
        return lax.dynamic_index_in_dim(v, home_turn, 1, keepdims=False)

    attended = to_order(merge(o_got[..., 64:], turned(o_got[..., :64])))
    attended = jnp.concatenate([attended, swap(attended)], axis=0)
    branch = nn(attended, out_w)
    mine, theirs = branch[:128], swap(branch[128:])
    f0, f1 = both(mine[:, :272], theirs[:, :272])
    f2, f3 = both(mine[:, 272:], theirs[:, 272:])
    middle = tokens_f + jnp.concatenate([f0, f1, f2, f3], axis=1) + branch_bias
    second_hat, second_inverse = standardize(middle)
    second = to_order((second_hat * gain_two + bias_two).astype(BF16))
    second = jnp.concatenate([second, swap(second)], axis=0)
    hidden = nn(second, fc) + hidden_bias
    active, gelu_pull = jax.vjp(lambda h: jax.nn.gelu(h, approximate=True), hidden)
    active = lax.reduce_precision(active, 8, 7).astype(BF16)
    final = nn(active, proj)
    final = final[:128] + swap(final[128:]) + final_bias
    layer_out = (mask * (middle + final)).astype(BF16)

    grad_out_low = jnp.where(valid, slots[1], BF16(0))
    grad_out = grad_out_low.astype(F32)
    grad_out_two = jnp.concatenate([grad_out_low, swap(grad_out_low)], axis=0)
    (grad_hidden,) = gelu_pull(nt(grad_out_two, proj))
    grad_hidden = lax.reduce_precision(grad_hidden, 8, 7)
    hidden_sum = jnp.sum(grad_hidden, axis=0)
    grad_hidden = grad_hidden.astype(BF16)
    g_proj = tn(active, grad_out_two).astype(BF16).reshape(16, 136, d)
    grad_second = nt(grad_hidden, fc)
    grad_second = from_order_wide(grad_second[:128] + swap(grad_second[128:]))
    g_fc = [tn(second, grad_hidden[:, i * d : i * d + d]).astype(BF16).reshape(16, PIECE, d) for i in range(2)]
    grad_mid, g_ln2_gain, g_ln2_bias = norm_back(grad_second, second_hat, second_inverse, gain_two)
    grad_middle = grad_out + grad_mid
    grad_branch = lax.reduce_precision(grad_middle, 8, 7)
    branch_sum = jnp.sum(grad_branch, axis=0)
    grad_branch = grad_branch.astype(BF16)
    both_branch = jnp.concatenate([grad_branch, swap(grad_branch)], axis=0)
    both_branch = jnp.concatenate(
        [
            jnp.where(even, both_branch[:, :272], both_branch[:, 272:544]),
            jnp.where(even, both_branch[:, 544:816], both_branch[:, 816:]),
        ],
        axis=1,
    )
    grad_attn = nt(both_branch, out_w)
    grad_attn = (grad_attn[:128] + swap(grad_attn[128:])).astype(BF16)
    grad_attn = from_order(grad_attn).astype(BF16)
    g_out = jnp.pad(tn(attended, both_branch).astype(BF16).reshape(16, PIECE, 544), ((0, 0), (0, 0), (0, 544)))
    packed = jnp.concatenate(g_fc + [g_out, g_proj], axis=1)
    packed = lax.psum_scatter(packed, YZ, scatter_dimension=0, tiled=True)[0]

    g = heads(grad_attn)
    ga = lax.all_to_all(pairs_of((every(g), g[:, first])), CTX, split_axis=0, concat_axis=0, tiled=True)
    ga = ga[own]
    g_all = ga[:, :, 64:].reshape(2048, 64)
    pair_g = jnp.concatenate([take(ga, turn)[:, :64], take(ga, 31 - turn)[:, :64]], axis=0)
    dqs = []
    dk = [jnp.zeros((2048, 64), F32), jnp.zeros((2048, 64), F32)]
    dv = [jnp.zeros((2048, 64), F32), jnp.zeros((2048, 64), F32)]
    for (r, n, keys, values, limit, at, q), (out, lse) in zip(tiles, outs):
        dq, dk_part, dv_part = tile_back(q, keys, values, limit, at, g_all[r], out, lse)
        dqs.append(dq)
        rows = n.stop
        for i in range(2):
            grow = ((0, 2048 - rows), (0, 0))
            dk[i] = dk[i] + jnp.pad(dk_part[i * rows : i * rows + rows], grow)
            dv[i] = dv[i] + jnp.pad(dv_part[i * rows : i * rows + rows], grow)
    dq_16, dk_16, dv_16 = tile_back(pair_q, k_16, v_16, pair_limit, at_all, pair_g, out_16, lse_16)
    dq_16 = dq_16.reshape(2, 64, 64)
    wide = jnp.where(is_turn == turn, dq_16[0], jnp.where(is_turn == 31 - turn, dq_16[1], 0.0))
    dq = jnp.concatenate([jnp.concatenate(dqs, axis=0).reshape(32, 64, 64), wide], axis=2).astype(BF16)
    mine = jnp.concatenate([dk[0], dv[0], dv_16[:2048], dk_16[:2048]], axis=1)
    theirs = jnp.concatenate([dk[1], dv[1], dv_16[2048:], dk_16[2048:]], axis=1).astype(BF16)
    total = (mine + swap(theirs).astype(F32)).astype(BF16).reshape(32, 64, 256)
    sent = jnp.concatenate([dq, total[:, :, :128], total[:, :, 128:]], axis=1)[inverse]
    got = lax.all_to_all(sent, CTX, split_axis=0, concat_axis=0, tiled=True)
    got = got.reshape(2, 16, 192, 128)
    last = jnp.sum(got[:, :, 128:].astype(F32), axis=1).astype(BF16)
    grad_projected = jnp.concatenate(
        [
            merge(got[:, :, :64, :64], turned(got[:, :, :64, 64:])),
            merge(got[:, :, 64:128, :64], last[:, :, 64:]),
            merge(got[:, :, 64:128, 64:], last[:, :, :64]),
        ],
        axis=1,
    )
    columns_sum = jnp.sum(grad_projected.astype(F32), axis=0)
    f0, f1 = both(grad_projected[:, :816], grad_projected[:, 816:1632])
    f2, f3 = both(grad_projected[:, 1632:2448], grad_projected[:, 2448:])
    part_a = jnp.concatenate([f0, swap(f1)], axis=0)
    part_b = jnp.concatenate([f2, swap(f3)], axis=0)
    g_a = tn(normed, part_a).astype(BF16).reshape(4, 4 * PIECE, 816)
    g_b = tn(normed, part_b).astype(BF16).reshape(4, 4, PIECE, 816)
    g_a = sum_ring(g_a, "y", y).astype(BF16)
    g_b = sum_ring(g_b, "z", z, 1).astype(BF16)
    g_a = sum_ring(g_a.reshape(4, PIECE, 816), "z", z).astype(BF16)
    g_b = sum_ring(g_b, "y", y).astype(BF16)
    g_qkv = jnp.stack([g_a[:34], g_a[34:68], g_b[:34], g_b[34:68]])
    qkv_sum = sum_ring(g_qkv, X, x)
    grad_normed = nt(part_a, qkv_a) + nt(part_b, qkv_b)
    grad_normed = from_order_wide(grad_normed[:128] + swap(grad_normed[128:]))
    grad_in, g_ln1_gain, g_ln1_bias = norm_back(grad_normed, first_hat, first_inverse, gain_one)
    grad_tokens = (grad_middle + grad_in).astype(BF16)

    results = jnp.stack([layer_out, grad_tokens])
    first, last = results[:, :64], results[:, 64:]
    home = jnp.where(even, first, last)
    away = swap(jnp.where(even, last, first))
    placed = jnp.concatenate([jnp.where(low, home, away), jnp.where(low, away, home)], axis=1)

    fc_rows = jnp.concatenate([packed[:PIECE], packed[PIECE : 2 * PIECE]], axis=1)
    out_rows = packed[2 * PIECE : 3 * PIECE, :544]
    proj_rows = packed[3 * PIECE :]
    proj_x = jnp.stack([proj_rows[:, i * 272 : i * 272 + 272] for i in range(4)])
    proj_sum = sum_ring(proj_x, X, x)
    proj_sum = lax.ppermute(proj_sum, ("co", "xl"), [(0, 0), (1, 2), (2, 1), (3, 3)])
    fc_x = jnp.concatenate([x_of_rows(fc_rows), x_of_rows(out_rows)], axis=2)
    fc_sum = sum_ring(fc_x, X, x)
    out_sum = fc_sum[:, 1088:]
    h0, h1 = both(fc_sum[:, :544], fc_sum[:, 544:1088])
    h0, h1 = both(h0, swap(h1))
    fc_sum = jnp.concatenate([h0, h1], axis=1)

    g_hidden_bias = hidden_sum.reshape(4, 1, 544)
    zero = jnp.zeros_like(g_hidden_bias)
    g_hidden_bias = jnp.concatenate(both(g_hidden_bias, zero), axis=1).reshape(32, 136)
    sums = [
        g_ln1_gain,
        g_ln1_bias,
        columns_sum[:d],
        columns_sum[2 * d :],
        branch_sum,
        g_ln2_gain,
        g_ln2_bias,
        jnp.sum(grad_out, axis=0),
    ]
    sums = jnp.concatenate([v.reshape(32, 34) for v in sums] + [g_hidden_bias], axis=1)
    sums = sums + swap(sums)
    sums = sums + lax.ppermute(sums, "xh", SWAP)
    sums = lax.all_to_all(sums, CTX, split_axis=0, concat_axis=0, tiled=True)
    sums = jnp.sum(sums, axis=0)
    v = [sums[34 * i : 34 * i + 34] for i in range(8)]
    return (
        placed[0][None],
        placed[1][None],
        v[0],
        v[1],
        qkv_sum,
        v[2],
        v[3],
        out_sum,
        v[4],
        v[5],
        v[6],
        fc_sum,
        sums[272:],
        proj_sum,
        v[7],
    )


def solution(mesh):
    grid = Mesh(mesh.devices.reshape(2, 2, 4, 2, 4), AXES)
    f = ("xh", "co")
    rows = P(f, CTX, None)
    matrix = P(CTX, f)
    vector = P(CTX)
    ins = (rows, rows, P(f), P(), vector, vector, matrix, vector, vector, matrix)
    ins = ins + (vector, vector, vector, matrix, vector, matrix, vector)
    outs = (rows, rows, vector, vector, matrix, vector, vector, matrix, vector, vector, vector)
    outs = outs + (matrix, vector, matrix, vector)
    return jax.shard_map(body, mesh=grid, in_specs=ins, out_specs=outs, check_vma=False)
```

```python
import jax
import jax.numpy as jnp
import numpy as np
from jax import lax
from jax.sharding import Mesh
from jax.sharding import PartitionSpec as P

F32 = jnp.float32
BF16 = jnp.bfloat16
HD = 64
SCALE = HD**-0.5
NEG = -1e30
AXES = ("xh", "co", "y", "xl", "z")
CTX = ("y", "xl", "z")
YZ = ("y", "z")
X = ("xh", "xl")
SWAP = [(0, 1), (1, 0)]

PIECE = 72
ORDER = np.full((16, PIECE), -1, np.int32)
for _n in range(16):
    for _xl in range(2):
        _c = (_n // 4) * 8 + _xl * 4 + _n % 4
        ORDER[_n, _xl * 34 : _xl * 34 + 34] = _c * 34 + np.arange(34)
ORDER = ORDER.reshape(-1)
DP = 16 * PIECE


def ring(n, s):
    return [(i, (i + s) % n) for i in range(n)]


def swap(v):
    return lax.ppermute(v, "co", SWAP)


def nt(a, b):
    return lax.dot_general(a, b, (((1,), (1,)), ((), ())), preferred_element_type=F32)


def nn(a, b):
    return lax.dot_general(a, b, (((1,), (0,)), ((), ())), preferred_element_type=F32)


def tn(a, b):
    return lax.dot_general(a, b, (((0,), (0,)), ((), ())), preferred_element_type=F32)


def heads(v):
    return jnp.transpose(v.reshape(2, 64, 17, 64), (0, 2, 1, 3))


def every(v):
    return jnp.broadcast_to(v[:, 16:], (2, 16, 64, 64))


def pairs_of(*parts):
    rows = [jnp.concatenate(pair, axis=3) for pair in parts]
    return jnp.concatenate(rows, axis=2).reshape(32, 64 * len(parts), 128)


def merge(first, last):
    whole = jnp.concatenate([first, last[:, None]], axis=1)
    return jnp.transpose(whole, (0, 2, 1, 3)).reshape(128, 1088)


def take(v, i):
    return lax.dynamic_index_in_dim(v, i, 0, keepdims=False)


def tile_attend(q, k, v, limit, at):
    s = jnp.where(at[:, None] <= limit[None, :], nt(k, q) * SCALE, NEG)
    top = jnp.max(s, axis=0, keepdims=True)
    e = jnp.exp(s - top)
    total = jnp.sum(e, axis=0, keepdims=True)
    out = tn(v, e.astype(BF16)) / total
    return out, top + jnp.log(total)


def tile_back(q, k, v, limit, at, g, out, lse):
    s = jnp.where(at[:, None] <= limit[None, :], nt(k, q) * SCALE, NEG)
    e = jnp.exp(s - lse)
    delta = jnp.sum(g.astype(F32).T * out, axis=0, keepdims=True)
    ds = (e * (nt(v, g) - delta)).astype(BF16)
    return tn(ds, k) * SCALE, nn(ds, q) * SCALE, nn(e.astype(BF16), g)


def standardize(values):
    center = values - jnp.mean(values, axis=-1, keepdims=True)
    spread = jnp.mean(center * center, axis=-1, keepdims=True)
    inverse = lax.rsqrt(spread + 1e-05)
    return (center * inverse, inverse)


def norm_back(grad_result, hat, inverse, gain):
    scaled = grad_result * gain
    first = jnp.mean(scaled, axis=-1, keepdims=True)
    second = jnp.mean(scaled * hat, axis=-1, keepdims=True)
    grad_input = inverse * (scaled - first - hat * second)
    return (grad_input, jnp.sum(grad_result * hat, axis=0), jnp.sum(grad_result, axis=0))


def order_matrix():
    order = jnp.asarray(ORDER)
    return (jnp.arange(16 * 68)[:, None] == order[None, :]).astype(BF16)


def to_order(v):
    return nn(v, order_matrix()).astype(BF16)


def from_order(v):
    return nt(v, order_matrix())


def from_order_wide(v):
    high = lax.reduce_precision(v, 8, 7)
    return from_order(high.astype(BF16)) + from_order((v - high).astype(BF16))


def gather_ring(piece, axis, at):
    out = jnp.zeros((4,) + piece.shape, piece.dtype)
    out = lax.dynamic_update_index_in_dim(out, piece, at, 0)
    for s in (1, 3, 2):
        got = lax.ppermute(piece, axis, ring(4, s))
        out = lax.dynamic_update_index_in_dim(out, got, (at + 4 - s) % 4, 0)
    return out


def sum_ring(pieces, axis, at, dim=0):
    total = lax.dynamic_index_in_dim(pieces, at, dim, keepdims=False).astype(F32)
    for s in (1, 3, 2):
        part = lax.dynamic_index_in_dim(pieces, (at + s) % 4, dim, keepdims=False)
        total = total + lax.ppermute(part, axis, ring(4, s)).astype(F32)
    return total


def rows_of_x(four):
    top = jnp.concatenate([four[0], four[2]], axis=1)
    low = jnp.concatenate([four[1], four[3]], axis=1)
    return jnp.concatenate([top, low, jnp.zeros((4, top.shape[1]), top.dtype)], axis=0)


def x_of_rows(rows):
    n = rows.shape[1] // 2
    return jnp.stack([rows[:34, :n], rows[34:68, :n], rows[:34, n:], rows[34:68, n:]])


def body(
    tokens,
    cotangent,
    lengths,
    block_order,
    ln1_gain,
    ln1_bias,
    w_qkv,
    q_bias,
    v_bias,
    w_out,
    out_bias,
    ln2_gain,
    ln2_bias,
    w_fc,
    fc_bias,
    w_proj,
    proj_bias,
):
    d = 1088
    xh, co, y, xl, z = (lax.axis_index(a) for a in AXES)
    ctx = y * 8 + xl * 4 + z
    x = xh * 2 + xl
    even = co == 0

    def both(own, other):
        return jnp.where(even, own, other), jnp.where(even, other, own)

    qkv_piece = rows_of_x(gather_ring(w_qkv, X, x))
    w_fc, w_out, w_proj, qkv_piece = lax.optimization_barrier((w_fc, w_out, w_proj, qkv_piece))
    qkv = lax.all_gather(qkv_piece, YZ, axis=0, tiled=True)
    fc_keep, fc_half = both(w_fc[:, :544], w_fc[:, 544:])
    fc_own = jnp.concatenate(both(fc_keep, swap(fc_half)), axis=1)
    proj_own = lax.ppermute(w_proj, ("co", "xl"), [(0, 0), (1, 2), (2, 1), (3, 3)])
    four = gather_ring(jnp.concatenate([w_out, fc_own], axis=1), X, x)
    fc_piece = jnp.concatenate([rows_of_x(four[:, :, 272:]), rows_of_x(four[:, :, :272])], axis=1)
    four = gather_ring(proj_own, X, x)
    proj_piece = jnp.concatenate([four[0], four[1], four[2], four[3]], axis=1)
    fc_piece, proj_piece, qkv = lax.optimization_barrier((fc_piece, proj_piece, qkv))
    fc_out = lax.all_gather(fc_piece, YZ, axis=0, tiled=True)
    proj = lax.all_gather(proj_piece, YZ, axis=0, tiled=True)
    fc = fc_out[:, :2176]
    out_w = fc_out[:, 2176:]

    vectors = jnp.concatenate(
        [ln1_gain, ln1_bias, q_bias, v_bias, out_bias, ln2_gain, ln2_bias, proj_bias, fc_bias]
    ).astype(F32)
    vectors = lax.all_to_all(
        jnp.broadcast_to(vectors[None], (32, 408)), CTX, split_axis=0, concat_axis=0, tiled=True
    )
    gain_one, bias_one, query_bias, value_bias, branch_bias, gain_two, bias_two, final_bias = (
        vectors[:, 34 * i : 34 * i + 34].reshape(1, d) for i in range(8)
    )
    hidden_bias = vectors[:, 272:].reshape(4, 2, 544)
    hidden_bias = jnp.where(even, hidden_bias[:, 0], hidden_bias[:, 1]).reshape(1, 2176)

    pair = lax.dynamic_index_in_dim(block_order, ctx, 0, keepdims=False)
    keep = (co + pair) % 2
    sent = jnp.concatenate([tokens, cotangent], axis=0)
    low = keep == 0
    kept = jnp.where(low, sent[:, :64], sent[:, 64:])
    sent = jnp.where(low, sent[:, 64:], sent[:, :64])
    slots = jnp.stack(both(kept, swap(sent)), axis=1).reshape(2, 128, d)
    length = jnp.concatenate(both(lengths, swap(lengths)))
    block = jnp.where(keep == 0, pair, 63 - pair)
    at = block * 64 + jnp.arange(64, dtype=jnp.int32)
    valid = (at[None, :] < length[:, None]).reshape(128, 1)
    mask = valid.astype(F32)

    blocks = 2 * jnp.arange(32, dtype=jnp.int32)[None, :] + jnp.arange(2, dtype=jnp.int32)[:, None]
    pairs = jnp.where(blocks < 32, blocks, 63 - blocks)
    match = pairs[:, :, None] == block_order[None, None, :]
    found = jnp.sum(jnp.where(match, jnp.arange(32, dtype=jnp.int32), 0), axis=2).astype(jnp.int32)
    own = jnp.where(even, found[0], found[1])
    oth = jnp.where(even, found[1], found[0])
    index = (block - co) // 2
    info = jnp.stack(
        [co, ctx % 16, jnp.where(index < 16, index, 31 - index), jnp.where(ctx < 16, length[0], length[1])]
    ).astype(jnp.int32)

    tokens_f = slots[0].astype(F32)
    first_hat, first_inverse = standardize(tokens_f)
    normed = to_order((first_hat * gain_one + bias_one).astype(BF16))
    normed = jnp.concatenate([normed, swap(normed)], axis=0)
    bias = jnp.concatenate([query_bias, jnp.zeros((1, d), F32), value_bias], axis=1)
    bias_a = jnp.where(even, bias[:, :816], bias[:, 816:1632])
    bias_b = jnp.where(even, bias[:, 1632:2448], bias[:, 2448:])
    projected = (nn(normed, qkv) + jnp.concatenate([bias_a, bias_b], axis=1)).astype(BF16)
    mine, theirs = projected[:128], swap(projected[128:])
    f0, f1 = both(mine[:, :816], theirs[:, :816])
    f2, f3 = both(mine[:, 816:], theirs[:, 816:])
    whole = jnp.concatenate([f0, f1, f2, f3], axis=1)
    q, k, v = (heads(whole[:, i * d : i * d + d]) for i in range(3))
    first, last = slice(0, 16), slice(16, 17)
    sent = pairs_of((q[:, first], every(q)), (k[:, first], v[:, first]), (every(v), every(k)))
    xs = lax.all_to_all(sent, CTX, split_axis=0, concat_axis=0, tiled=True)
    xo = swap(xs[:, 64:])
    turn = info[1]
    xs, xo = xs[own], xo[oth]
    inner = jnp.arange(64, dtype=jnp.int32)
    at_q = ((2 * jnp.arange(32, dtype=jnp.int32) + co)[:, None] * 64 + inner).reshape(2048)
    at_o = ((2 * jnp.arange(32, dtype=jnp.int32) + 1 - co)[:, None] * 64 + inner).reshape(2048)
    q_all = xs[:, :64, :64].reshape(2048, 64)
    pair_q = jnp.concatenate([take(xs, turn)[:64, 64:], take(xs, 31 - turn)[:64, 64:]], axis=0)
    k_own, v_own = xs[:, 64:128, :64].reshape(2048, 64), xs[:, 64:128, 64:].reshape(2048, 64)
    k_oth, v_oth = xo[:, :64, :64].reshape(2048, 64), xo[:, :64, 64:].reshape(2048, 64)
    v_16 = jnp.concatenate([xs[:, 128:, :64].reshape(2048, 64), xo[:, 64:, :64].reshape(2048, 64)], axis=0)
    k_16 = jnp.concatenate([xs[:, 128:, 64:].reshape(2048, 64), xo[:, 64:, 64:].reshape(2048, 64)], axis=0)
    bound = info[3] - 1
    at_all = jnp.concatenate([at_q, at_o])
    at_pair = jnp.concatenate([take(at_q.reshape(32, 64), turn), take(at_q.reshape(32, 64), 31 - turn)])
    tiles = []
    for j in range(4):
        r, n = slice(512 * j, 512 * j + 512), slice(0, 512 * j + 512)
        keys = jnp.concatenate([k_own[n], k_oth[n]], axis=0)
        values = jnp.concatenate([v_own[n], v_oth[n]], axis=0)
        at = jnp.concatenate([at_q[n], at_o[n]])
        limit = jnp.minimum(at_q[r], bound)
        tiles.append((r, n, keys, values, limit, at, q_all[r]))
    outs = [tile_attend(q, keys, values, limit, at) for r, n, keys, values, limit, at, q in tiles]
    pair_limit = jnp.minimum(at_pair, bound)
    out_16, lse_16 = tile_attend(pair_q, k_16, v_16, pair_limit, at_all)
    inverse = jnp.sum(jnp.where(own[None, :] == jnp.arange(32)[:, None], jnp.arange(32), 0), axis=1)
    is_turn = jnp.arange(32)[:, None, None]
    low_16 = out_16.T.reshape(2, 64, 64)
    wide = jnp.where(is_turn == turn, low_16[0], jnp.where(is_turn == 31 - turn, low_16[1], 0.0))
    low_all = jnp.concatenate([o.T for o, _ in outs], axis=0).reshape(32, 64, 64)
    o_sent = jnp.concatenate([wide, low_all], axis=2).astype(BF16)[inverse]
    o_got = lax.all_to_all(o_sent, CTX, split_axis=0, concat_axis=0, tiled=True)
    o_got = o_got.reshape(2, 16, 64, 128)
    home_turn = info[2]

    def turned(v):
        return lax.dynamic_index_in_dim(v, home_turn, 1, keepdims=False)

    attended = to_order(merge(o_got[..., 64:], turned(o_got[..., :64])))
    attended = jnp.concatenate([attended, swap(attended)], axis=0)
    branch = nn(attended, out_w)
    mine, theirs = branch[:128], swap(branch[128:])
    f0, f1 = both(mine[:, :272], theirs[:, :272])
    f2, f3 = both(mine[:, 272:], theirs[:, 272:])
    middle = tokens_f + jnp.concatenate([f0, f1, f2, f3], axis=1) + branch_bias
    second_hat, second_inverse = standardize(middle)
    second = to_order((second_hat * gain_two + bias_two).astype(BF16))
    second = jnp.concatenate([second, swap(second)], axis=0)
    hidden = nn(second, fc) + hidden_bias
    active, gelu_pull = jax.vjp(lambda h: jax.nn.gelu(h, approximate=True), hidden)
    active = lax.reduce_precision(active, 8, 7).astype(BF16)
    final = nn(active, proj)
    final = final[:128] + swap(final[128:]) + final_bias
    layer_out = (mask * (middle + final)).astype(BF16)

    grad_out_low = jnp.where(valid, slots[1], BF16(0))
    grad_out = grad_out_low.astype(F32)
    grad_out_two = jnp.concatenate([grad_out_low, swap(grad_out_low)], axis=0)
    (grad_hidden,) = gelu_pull(nt(grad_out_two, proj))
    grad_hidden = lax.reduce_precision(grad_hidden, 8, 7)
    hidden_sum = jnp.sum(grad_hidden, axis=0)
    grad_hidden = grad_hidden.astype(BF16)
    g_proj = tn(active, grad_out_two).astype(BF16).reshape(16, 136, d)
    grad_second = nt(grad_hidden, fc)
    grad_second = from_order_wide(grad_second[:128] + swap(grad_second[128:]))
    g_fc = [tn(second, grad_hidden[:, i * d : i * d + d]).astype(BF16).reshape(16, PIECE, d) for i in range(2)]
    grad_mid, g_ln2_gain, g_ln2_bias = norm_back(grad_second, second_hat, second_inverse, gain_two)
    grad_middle = grad_out + grad_mid
    grad_branch = lax.reduce_precision(grad_middle, 8, 7)
    branch_sum = jnp.sum(grad_branch, axis=0)
    grad_branch = grad_branch.astype(BF16)
    both_branch = jnp.concatenate([grad_branch, swap(grad_branch)], axis=0)
    both_branch = jnp.concatenate(
        [
            jnp.where(even, both_branch[:, :272], both_branch[:, 272:544]),
            jnp.where(even, both_branch[:, 544:816], both_branch[:, 816:]),
        ],
        axis=1,
    )
    grad_attn = nt(both_branch, out_w)
    grad_attn = (grad_attn[:128] + swap(grad_attn[128:])).astype(BF16)
    grad_attn = from_order(grad_attn).astype(BF16)
    g_out = jnp.pad(tn(attended, both_branch).astype(BF16).reshape(16, PIECE, 544), ((0, 0), (0, 0), (0, 544)))
    packed = jnp.concatenate(g_fc + [g_out, g_proj], axis=1)
    packed = lax.psum_scatter(packed.reshape(16 * 352, d), YZ, scatter_dimension=0, tiled=True)
    packed = lax.optimization_barrier(packed)

    g = heads(grad_attn)
    ga = lax.all_to_all(pairs_of((every(g), g[:, first])), CTX, split_axis=0, concat_axis=0, tiled=True)
    ga = ga[own]
    g_all = ga[:, :, 64:].reshape(2048, 64)
    pair_g = jnp.concatenate([take(ga, turn)[:, :64], take(ga, 31 - turn)[:, :64]], axis=0)
    dqs = []
    dk = [jnp.zeros((2048, 64), F32), jnp.zeros((2048, 64), F32)]
    dv = [jnp.zeros((2048, 64), F32), jnp.zeros((2048, 64), F32)]
    for (r, n, keys, values, limit, at, q), (out, lse) in zip(tiles, outs):
        dq, dk_part, dv_part = tile_back(q, keys, values, limit, at, g_all[r], out, lse)
        dqs.append(dq)
        rows = n.stop
        for i in range(2):
            grow = ((0, 2048 - rows), (0, 0))
            dk[i] = dk[i] + jnp.pad(dk_part[i * rows : i * rows + rows], grow)
            dv[i] = dv[i] + jnp.pad(dv_part[i * rows : i * rows + rows], grow)
    dq_16, dk_16, dv_16 = tile_back(pair_q, k_16, v_16, pair_limit, at_all, pair_g, out_16, lse_16)
    dq_16 = dq_16.reshape(2, 64, 64)
    wide = jnp.where(is_turn == turn, dq_16[0], jnp.where(is_turn == 31 - turn, dq_16[1], 0.0))
    dq = jnp.concatenate([jnp.concatenate(dqs, axis=0).reshape(32, 64, 64), wide], axis=2).astype(BF16)
    mine = jnp.concatenate([dk[0], dv[0], dv_16[:2048], dk_16[:2048]], axis=1)
    theirs = jnp.concatenate([dk[1], dv[1], dv_16[2048:], dk_16[2048:]], axis=1).astype(BF16)
    total = (mine + swap(theirs).astype(F32)).astype(BF16).reshape(32, 64, 256)
    sent = jnp.concatenate([dq, total[:, :, :128], total[:, :, 128:]], axis=1)[inverse]
    got = lax.all_to_all(sent, CTX, split_axis=0, concat_axis=0, tiled=True)
    got = got.reshape(2, 16, 192, 128)
    last = jnp.sum(got[:, :, 128:].astype(F32), axis=1).astype(BF16)
    grad_projected = jnp.concatenate(
        [
            merge(got[:, :, :64, :64], turned(got[:, :, :64, 64:])),
            merge(got[:, :, 64:128, :64], last[:, :, 64:]),
            merge(got[:, :, 64:128, 64:], last[:, :, :64]),
        ],
        axis=1,
    )
    columns_sum = jnp.sum(grad_projected.astype(F32), axis=0)
    f0, f1 = both(grad_projected[:, :816], grad_projected[:, 816:1632])
    f2, f3 = both(grad_projected[:, 1632:2448], grad_projected[:, 2448:])
    part_a = jnp.concatenate([f0, swap(f1)], axis=0)
    part_b = jnp.concatenate([f2, swap(f3)], axis=0)
    g_a = tn(normed, part_a).astype(BF16).reshape(4, 4 * PIECE, 816)
    g_b = tn(normed, part_b).astype(BF16).reshape(4, 4, PIECE, 816)
    g_a = sum_ring(g_a, "y", y).astype(BF16)
    g_b = sum_ring(g_b, "z", z, 1).astype(BF16)
    g_a = sum_ring(g_a.reshape(4, PIECE, 816), "z", z).astype(BF16)
    g_b = sum_ring(g_b, "y", y).astype(BF16)
    g_qkv = jnp.stack([g_a[:34], g_a[34:68], g_b[:34], g_b[34:68]])
    qkv_sum = sum_ring(g_qkv, X, x)
    grad_normed = nt(jnp.concatenate([part_a, part_b], axis=1), qkv)
    grad_normed = from_order_wide(grad_normed[:128] + swap(grad_normed[128:]))
    grad_in, g_ln1_gain, g_ln1_bias = norm_back(grad_normed, first_hat, first_inverse, gain_one)
    grad_tokens = (grad_middle + grad_in).astype(BF16)

    results = jnp.stack([layer_out, grad_tokens])
    first, last = results[:, :64], results[:, 64:]
    home = jnp.where(even, first, last)
    away = swap(jnp.where(even, last, first))
    placed = jnp.concatenate([jnp.where(low, home, away), jnp.where(low, away, home)], axis=1)

    fc_rows = jnp.concatenate([packed[:PIECE], packed[PIECE : 2 * PIECE]], axis=1)
    out_rows = packed[2 * PIECE : 3 * PIECE, :544]
    proj_rows = packed[3 * PIECE :]
    proj_x = jnp.stack([proj_rows[:, i * 272 : i * 272 + 272] for i in range(4)])
    proj_sum = sum_ring(proj_x, X, x)
    proj_sum = lax.ppermute(proj_sum, ("co", "xl"), [(0, 0), (1, 2), (2, 1), (3, 3)])
    fc_x = jnp.concatenate([x_of_rows(fc_rows), x_of_rows(out_rows)], axis=2)
    fc_sum = sum_ring(fc_x, X, x)
    out_sum = fc_sum[:, 1088:]
    h0, h1 = both(fc_sum[:, :544], fc_sum[:, 544:1088])
    h0, h1 = both(h0, swap(h1))
    fc_sum = jnp.concatenate([h0, h1], axis=1)

    g_hidden_bias = hidden_sum.reshape(4, 1, 544)
    zero = jnp.zeros_like(g_hidden_bias)
    g_hidden_bias = jnp.concatenate(both(g_hidden_bias, zero), axis=1).reshape(32, 136)
    sums = [
        g_ln1_gain,
        g_ln1_bias,
        columns_sum[:d],
        columns_sum[2 * d :],
        branch_sum,
        g_ln2_gain,
        g_ln2_bias,
        jnp.sum(grad_out, axis=0),
    ]
    sums = jnp.concatenate([v.reshape(32, 34) for v in sums] + [g_hidden_bias], axis=1)
    sums = sums + swap(sums)
    sums = sums + lax.ppermute(sums, "xh", SWAP)
    sums = lax.all_to_all(sums, CTX, split_axis=0, concat_axis=0, tiled=True)
    sums = jnp.sum(sums, axis=0)
    v = [sums[34 * i : 34 * i + 34] for i in range(8)]
    return (
        placed[0][None],
        placed[1][None],
        v[0],
        v[1],
        qkv_sum,
        v[2],
        v[3],
        out_sum,
        v[4],
        v[5],
        v[6],
        fc_sum,
        sums[272:],
        proj_sum,
        v[7],
    )


def solution(mesh):
    grid = Mesh(mesh.devices.reshape(2, 2, 4, 2, 4), AXES)
    f = ("xh", "co")
    rows = P(f, CTX, None)
    matrix = P(CTX, f)
    vector = P(CTX)
    ins = (rows, rows, P(f), P(), vector, vector, matrix, vector, vector, matrix)
    ins = ins + (vector, vector, vector, matrix, vector, matrix, vector)
    outs = (rows, rows, vector, vector, matrix, vector, vector, matrix, vector, vector, vector)
    outs = outs + (matrix, vector, matrix, vector)
    return jax.shard_map(body, mesh=grid, in_specs=ins, out_specs=outs, check_vma=False)
```

```python
import jax
import jax.numpy as jnp
import numpy as np
from jax import lax
from jax.sharding import Mesh
from jax.sharding import PartitionSpec as P

F32 = jnp.float32
BF16 = jnp.bfloat16
HD = 64
SCALE = HD**-0.5
NEG = -1e30
AXES = ("xh", "co", "y", "xl", "z")
CTX = ("y", "xl", "z")
YZ = ("y", "z")
X = ("xh", "xl")
SWAP = [(0, 1), (1, 0)]

PIECE = 72
ORDER = np.full((16, PIECE), -1, np.int32)
for _n in range(16):
    for _xl in range(2):
        _c = (_n // 4) * 8 + _xl * 4 + _n % 4
        ORDER[_n, _xl * 34 : _xl * 34 + 34] = _c * 34 + np.arange(34)
ORDER = ORDER.reshape(-1)
DP = 16 * PIECE


def ring(n, s):
    return [(i, (i + s) % n) for i in range(n)]


def swap(v):
    return lax.ppermute(v, "co", SWAP)


def nt(a, b):
    return lax.dot_general(a, b, (((1,), (1,)), ((), ())), preferred_element_type=F32)


def nn(a, b):
    return lax.dot_general(a, b, (((1,), (0,)), ((), ())), preferred_element_type=F32)


def tn(a, b):
    return lax.dot_general(a, b, (((0,), (0,)), ((), ())), preferred_element_type=F32)


def heads(v):
    return jnp.transpose(v.reshape(2, 64, 17, 64), (0, 2, 1, 3))


def every(v):
    return jnp.broadcast_to(v[:, 16:], (2, 16, 64, 64))


def pairs_of(*parts):
    rows = [jnp.concatenate(pair, axis=3) for pair in parts]
    return jnp.concatenate(rows, axis=2).reshape(32, 64 * len(parts), 128)


def merge(first, last):
    whole = jnp.concatenate([first, last[:, None]], axis=1)
    return jnp.transpose(whole, (0, 2, 1, 3)).reshape(128, 1088)


def take(v, i):
    return lax.dynamic_index_in_dim(v, i, 0, keepdims=False)


def tile_attend(q, k, v, limit, at):
    s = jnp.where(at[:, None] <= limit[None, :], nt(k, q) * SCALE, NEG)
    top = jnp.max(s, axis=0, keepdims=True)
    e = jnp.exp(s - top)
    total = jnp.sum(e, axis=0, keepdims=True)
    out = tn(v, e.astype(BF16)) / total
    return out, top + jnp.log(total)


def tile_back(q, k, v, limit, at, g, out, lse):
    s = jnp.where(at[:, None] <= limit[None, :], nt(k, q) * SCALE, NEG)
    e = jnp.exp(s - lse)
    delta = jnp.sum(g.astype(F32).T * out, axis=0, keepdims=True)
    ds = (e * (nt(v, g) - delta)).astype(BF16)
    return tn(ds, k) * SCALE, nn(ds, q) * SCALE, nn(e.astype(BF16), g)


def standardize(values):
    center = values - jnp.mean(values, axis=-1, keepdims=True)
    spread = jnp.mean(center * center, axis=-1, keepdims=True)
    inverse = lax.rsqrt(spread + 1e-05)
    return (center * inverse, inverse)


def norm_back(grad_result, hat, inverse, gain):
    scaled = grad_result * gain
    first = jnp.mean(scaled, axis=-1, keepdims=True)
    second = jnp.mean(scaled * hat, axis=-1, keepdims=True)
    grad_input = inverse * (scaled - first - hat * second)
    return (grad_input, jnp.sum(grad_result * hat, axis=0), jnp.sum(grad_result, axis=0))


def order_matrix():
    order = jnp.asarray(ORDER)
    return (jnp.arange(16 * 68)[:, None] == order[None, :]).astype(BF16)


def to_order(v):
    return nn(v, order_matrix()).astype(BF16)


def from_order(v):
    return nt(v, order_matrix())


def from_order_wide(v):
    high = lax.reduce_precision(v, 8, 7)
    return from_order(high.astype(BF16)) + from_order((v - high).astype(BF16))


def gather_ring(piece, axis, at):
    out = jnp.zeros((4,) + piece.shape, piece.dtype)
    out = lax.dynamic_update_index_in_dim(out, piece, at, 0)
    for s in (1, 3, 2):
        got = lax.ppermute(piece, axis, ring(4, s))
        out = lax.dynamic_update_index_in_dim(out, got, (at + 4 - s) % 4, 0)
    return out


def sum_ring(pieces, axis, at, dim=0):
    total = lax.dynamic_index_in_dim(pieces, at, dim, keepdims=False).astype(F32)
    for s in (1, 3, 2):
        part = lax.dynamic_index_in_dim(pieces, (at + s) % 4, dim, keepdims=False)
        total = total + lax.ppermute(part, axis, ring(4, s)).astype(F32)
    return total


def rows_of_x(four):
    top = jnp.concatenate([four[0], four[2]], axis=1)
    low = jnp.concatenate([four[1], four[3]], axis=1)
    return jnp.concatenate([top, low, jnp.zeros((4, top.shape[1]), top.dtype)], axis=0)


def x_of_rows(rows):
    n = rows.shape[1] // 2
    return jnp.stack([rows[:34, :n], rows[34:68, :n], rows[:34, n:], rows[34:68, n:]])


def body(
    tokens,
    cotangent,
    lengths,
    block_order,
    ln1_gain,
    ln1_bias,
    w_qkv,
    q_bias,
    v_bias,
    w_out,
    out_bias,
    ln2_gain,
    ln2_bias,
    w_fc,
    fc_bias,
    w_proj,
    proj_bias,
):
    d = 1088
    xh, co, y, xl, z = (lax.axis_index(a) for a in AXES)
    ctx = y * 8 + xl * 4 + z
    x = xh * 2 + xl
    even = co == 0

    def both(own, other):
        return jnp.where(even, own, other), jnp.where(even, other, own)

    qkv_piece = rows_of_x(gather_ring(w_qkv, X, x))
    vectors = jnp.concatenate(
        [ln1_gain, ln1_bias, q_bias, v_bias, out_bias, ln2_gain, ln2_bias, proj_bias, fc_bias]
    ).astype(F32)
    vectors, qkv_piece = lax.optimization_barrier((vectors, qkv_piece))
    vectors = lax.all_to_all(
        jnp.broadcast_to(vectors[None], (32, 408)), CTX, split_axis=0, concat_axis=0, tiled=True
    )
    qkv = lax.all_gather(qkv_piece, YZ, axis=0, tiled=True)
    w_fc, w_out, w_proj, vectors = lax.optimization_barrier((w_fc, w_out, w_proj, vectors))
    fc_keep, fc_half = both(w_fc[:, :544], w_fc[:, 544:])
    fc_own = jnp.concatenate(both(fc_keep, swap(fc_half)), axis=1)
    proj_own = lax.ppermute(w_proj, ("co", "xl"), [(0, 0), (1, 2), (2, 1), (3, 3)])
    four = gather_ring(jnp.concatenate([w_out, fc_own], axis=1), X, x)
    fc_piece = jnp.concatenate([rows_of_x(four[:, :, 272:]), rows_of_x(four[:, :, :272])], axis=1)
    four = gather_ring(proj_own, X, x)
    proj_piece = jnp.concatenate([four[0], four[1], four[2], four[3]], axis=1)
    fc_piece, proj_piece, qkv = lax.optimization_barrier((fc_piece, proj_piece, qkv))
    fc_out = lax.all_gather(fc_piece, YZ, axis=0, tiled=True)
    proj = lax.all_gather(proj_piece, YZ, axis=0, tiled=True)
    fc = fc_out[:, :2176]
    out_w = fc_out[:, 2176:]

    gain_one, bias_one, query_bias, value_bias, branch_bias, gain_two, bias_two, final_bias = (
        vectors[:, 34 * i : 34 * i + 34].reshape(1, d) for i in range(8)
    )
    hidden_bias = vectors[:, 272:].reshape(4, 2, 544)
    hidden_bias = jnp.where(even, hidden_bias[:, 0], hidden_bias[:, 1]).reshape(1, 2176)

    pair = lax.dynamic_index_in_dim(block_order, ctx, 0, keepdims=False)
    keep = (co + pair) % 2
    sent = jnp.concatenate([tokens, cotangent], axis=0)
    low = keep == 0
    kept = jnp.where(low, sent[:, :64], sent[:, 64:])
    sent = jnp.where(low, sent[:, 64:], sent[:, :64])
    slots = jnp.stack(both(kept, swap(sent)), axis=1).reshape(2, 128, d)
    length = jnp.concatenate(both(lengths, swap(lengths)))
    block = jnp.where(keep == 0, pair, 63 - pair)
    at = block * 64 + jnp.arange(64, dtype=jnp.int32)
    valid = (at[None, :] < length[:, None]).reshape(128, 1)
    mask = valid.astype(F32)

    blocks = 2 * jnp.arange(32, dtype=jnp.int32)[None, :] + jnp.arange(2, dtype=jnp.int32)[:, None]
    pairs = jnp.where(blocks < 32, blocks, 63 - blocks)
    match = pairs[:, :, None] == block_order[None, None, :]
    found = jnp.sum(jnp.where(match, jnp.arange(32, dtype=jnp.int32), 0), axis=2).astype(jnp.int32)
    own = jnp.where(even, found[0], found[1])
    oth = jnp.where(even, found[1], found[0])
    index = (block - co) // 2
    info = jnp.stack(
        [co, ctx % 16, jnp.where(index < 16, index, 31 - index), jnp.where(ctx < 16, length[0], length[1])]
    ).astype(jnp.int32)

    tokens_f = slots[0].astype(F32)
    first_hat, first_inverse = standardize(tokens_f)
    normed = to_order((first_hat * gain_one + bias_one).astype(BF16))
    normed = jnp.concatenate([normed, swap(normed)], axis=0)
    bias = jnp.concatenate([query_bias, jnp.zeros((1, d), F32), value_bias], axis=1)
    bias_a = jnp.where(even, bias[:, :816], bias[:, 816:1632])
    bias_b = jnp.where(even, bias[:, 1632:2448], bias[:, 2448:])
    projected = (nn(normed, qkv) + jnp.concatenate([bias_a, bias_b], axis=1)).astype(BF16)
    mine, theirs = projected[:128], swap(projected[128:])
    f0, f1 = both(mine[:, :816], theirs[:, :816])
    f2, f3 = both(mine[:, 816:], theirs[:, 816:])
    whole = jnp.concatenate([f0, f1, f2, f3], axis=1)
    q, k, v = (heads(whole[:, i * d : i * d + d]) for i in range(3))
    first, last = slice(0, 16), slice(16, 17)
    sent = pairs_of((q[:, first], every(q)), (k[:, first], v[:, first]), (every(v), every(k)))
    xs = lax.all_to_all(sent, CTX, split_axis=0, concat_axis=0, tiled=True)
    xo = swap(xs[:, 64:])
    turn = info[1]
    xs, xo = xs[own], xo[oth]
    inner = jnp.arange(64, dtype=jnp.int32)
    at_q = ((2 * jnp.arange(32, dtype=jnp.int32) + co)[:, None] * 64 + inner).reshape(2048)
    at_o = ((2 * jnp.arange(32, dtype=jnp.int32) + 1 - co)[:, None] * 64 + inner).reshape(2048)
    q_all = xs[:, :64, :64].reshape(2048, 64)
    pair_q = jnp.concatenate([take(xs, turn)[:64, 64:], take(xs, 31 - turn)[:64, 64:]], axis=0)
    k_own, v_own = xs[:, 64:128, :64].reshape(2048, 64), xs[:, 64:128, 64:].reshape(2048, 64)
    k_oth, v_oth = xo[:, :64, :64].reshape(2048, 64), xo[:, :64, 64:].reshape(2048, 64)
    v_16 = jnp.concatenate([xs[:, 128:, :64].reshape(2048, 64), xo[:, 64:, :64].reshape(2048, 64)], axis=0)
    k_16 = jnp.concatenate([xs[:, 128:, 64:].reshape(2048, 64), xo[:, 64:, 64:].reshape(2048, 64)], axis=0)
    bound = info[3] - 1
    at_all = jnp.concatenate([at_q, at_o])
    at_pair = jnp.concatenate([take(at_q.reshape(32, 64), turn), take(at_q.reshape(32, 64), 31 - turn)])
    tiles = []
    for j in range(4):
        r, n = slice(512 * j, 512 * j + 512), slice(0, 512 * j + 512)
        keys = jnp.concatenate([k_own[n], k_oth[n]], axis=0)
        values = jnp.concatenate([v_own[n], v_oth[n]], axis=0)
        at = jnp.concatenate([at_q[n], at_o[n]])
        limit = jnp.minimum(at_q[r], bound)
        tiles.append((r, n, keys, values, limit, at, q_all[r]))
    outs = [tile_attend(q, keys, values, limit, at) for r, n, keys, values, limit, at, q in tiles]
    pair_limit = jnp.minimum(at_pair, bound)
    out_16, lse_16 = tile_attend(pair_q, k_16, v_16, pair_limit, at_all)
    inverse = jnp.sum(jnp.where(own[None, :] == jnp.arange(32)[:, None], jnp.arange(32), 0), axis=1)
    is_turn = jnp.arange(32)[:, None, None]
    low_16 = out_16.T.reshape(2, 64, 64)
    wide = jnp.where(is_turn == turn, low_16[0], jnp.where(is_turn == 31 - turn, low_16[1], 0.0))
    low_all = jnp.concatenate([o.T for o, _ in outs], axis=0).reshape(32, 64, 64)
    o_sent = jnp.concatenate([wide, low_all], axis=2).astype(BF16)[inverse]
    o_got = lax.all_to_all(o_sent, CTX, split_axis=0, concat_axis=0, tiled=True)
    o_got = o_got.reshape(2, 16, 64, 128)
    home_turn = info[2]

    def turned(v):
        return lax.dynamic_index_in_dim(v, home_turn, 1, keepdims=False)

    attended = to_order(merge(o_got[..., 64:], turned(o_got[..., :64])))
    attended = jnp.concatenate([attended, swap(attended)], axis=0)
    branch = nn(attended, out_w)
    mine, theirs = branch[:128], swap(branch[128:])
    f0, f1 = both(mine[:, :272], theirs[:, :272])
    f2, f3 = both(mine[:, 272:], theirs[:, 272:])
    middle = tokens_f + jnp.concatenate([f0, f1, f2, f3], axis=1) + branch_bias
    second_hat, second_inverse = standardize(middle)
    second = to_order((second_hat * gain_two + bias_two).astype(BF16))
    second = jnp.concatenate([second, swap(second)], axis=0)
    hidden = nn(second, fc) + hidden_bias
    active, gelu_pull = jax.vjp(lambda h: jax.nn.gelu(h, approximate=True), hidden)
    active = lax.reduce_precision(active, 8, 7).astype(BF16)
    final = nn(active, proj)
    final = final[:128] + swap(final[128:]) + final_bias
    layer_out = (mask * (middle + final)).astype(BF16)

    grad_out_low = jnp.where(valid, slots[1], BF16(0))
    grad_out = grad_out_low.astype(F32)
    grad_out_two = jnp.concatenate([grad_out_low, swap(grad_out_low)], axis=0)
    (grad_hidden,) = gelu_pull(nt(grad_out_two, proj))
    grad_hidden = lax.reduce_precision(grad_hidden, 8, 7)
    hidden_sum = jnp.sum(grad_hidden, axis=0)
    grad_hidden = grad_hidden.astype(BF16)
    grad_second = nt(grad_hidden, fc)
    grad_second = from_order_wide(grad_second[:128] + swap(grad_second[128:]))
    grad_mid, g_ln2_gain, g_ln2_bias = norm_back(grad_second, second_hat, second_inverse, gain_two)
    grad_middle = grad_out + grad_mid
    grad_branch = lax.reduce_precision(grad_middle, 8, 7)
    branch_sum = jnp.sum(grad_branch, axis=0)
    grad_branch = grad_branch.astype(BF16)
    both_branch = jnp.concatenate([grad_branch, swap(grad_branch)], axis=0)
    both_branch = jnp.concatenate(
        [
            jnp.where(even, both_branch[:, :272], both_branch[:, 272:544]),
            jnp.where(even, both_branch[:, 544:816], both_branch[:, 816:]),
        ],
        axis=1,
    )
    grad_attn = nt(both_branch, out_w)
    grad_attn = (grad_attn[:128] + swap(grad_attn[128:])).astype(BF16)
    grad_attn = from_order(grad_attn).astype(BF16)
    g = heads(grad_attn)
    sent = pairs_of((every(g), g[:, first]))
    sent, active, grad_out_two, second, grad_hidden, attended, both_branch = lax.optimization_barrier(
        (sent, active, grad_out_two, second, grad_hidden, attended, both_branch)
    )
    ga = lax.all_to_all(sent, CTX, split_axis=0, concat_axis=0, tiled=True)
    g_proj = tn(active, grad_out_two).astype(BF16).reshape(16, 136, d)
    g_fc = [tn(second, grad_hidden[:, i * d : i * d + d]).astype(BF16).reshape(16, PIECE, d) for i in range(2)]
    g_out = jnp.pad(tn(attended, both_branch).astype(BF16).reshape(16, PIECE, 544), ((0, 0), (0, 0), (0, 544)))
    packed = jnp.concatenate(g_fc + [g_out, g_proj], axis=1)
    packed = lax.psum_scatter(packed.reshape(16 * 352, d), YZ, scatter_dimension=0, tiled=True)
    packed = lax.optimization_barrier(packed)
    ga = ga[own]
    g_all = ga[:, :, 64:].reshape(2048, 64)
    pair_g = jnp.concatenate([take(ga, turn)[:, :64], take(ga, 31 - turn)[:, :64]], axis=0)
    dqs = []
    dk = [jnp.zeros((2048, 64), F32), jnp.zeros((2048, 64), F32)]
    dv = [jnp.zeros((2048, 64), F32), jnp.zeros((2048, 64), F32)]
    for (r, n, keys, values, limit, at, q), (out, lse) in zip(tiles, outs):
        dq, dk_part, dv_part = tile_back(q, keys, values, limit, at, g_all[r], out, lse)
        dqs.append(dq)
        rows = n.stop
        for i in range(2):
            grow = ((0, 2048 - rows), (0, 0))
            dk[i] = dk[i] + jnp.pad(dk_part[i * rows : i * rows + rows], grow)
            dv[i] = dv[i] + jnp.pad(dv_part[i * rows : i * rows + rows], grow)
    dq_16, dk_16, dv_16 = tile_back(pair_q, k_16, v_16, pair_limit, at_all, pair_g, out_16, lse_16)
    dq_16 = dq_16.reshape(2, 64, 64)
    wide = jnp.where(is_turn == turn, dq_16[0], jnp.where(is_turn == 31 - turn, dq_16[1], 0.0))
    dq = jnp.concatenate([jnp.concatenate(dqs, axis=0).reshape(32, 64, 64), wide], axis=2).astype(BF16)
    mine = jnp.concatenate([dk[0], dv[0], dv_16[:2048], dk_16[:2048]], axis=1)
    theirs = jnp.concatenate([dk[1], dv[1], dv_16[2048:], dk_16[2048:]], axis=1).astype(BF16)
    total = (mine + swap(theirs).astype(F32)).astype(BF16).reshape(32, 64, 256)
    sent = jnp.concatenate([dq, total[:, :, :128], total[:, :, 128:]], axis=1)[inverse]
    got = lax.all_to_all(sent, CTX, split_axis=0, concat_axis=0, tiled=True)
    got = got.reshape(2, 16, 192, 128)
    last = jnp.sum(got[:, :, 128:].astype(F32), axis=1).astype(BF16)
    grad_projected = jnp.concatenate(
        [
            merge(got[:, :, :64, :64], turned(got[:, :, :64, 64:])),
            merge(got[:, :, 64:128, :64], last[:, :, 64:]),
            merge(got[:, :, 64:128, 64:], last[:, :, :64]),
        ],
        axis=1,
    )
    columns_sum = jnp.sum(grad_projected.astype(F32), axis=0)
    f0, f1 = both(grad_projected[:, :816], grad_projected[:, 816:1632])
    f2, f3 = both(grad_projected[:, 1632:2448], grad_projected[:, 2448:])
    part_a = jnp.concatenate([f0, swap(f1)], axis=0)
    part_b = jnp.concatenate([f2, swap(f3)], axis=0)
    fc_rows = jnp.concatenate([packed[:PIECE], packed[PIECE : 2 * PIECE]], axis=1)
    out_rows = packed[2 * PIECE : 3 * PIECE, :544]
    proj_rows = packed[3 * PIECE :]
    proj_x = jnp.stack([proj_rows[:, i * 272 : i * 272 + 272] for i in range(4)])
    proj_sum = sum_ring(proj_x, X, x)
    proj_sum = lax.ppermute(proj_sum, ("co", "xl"), [(0, 0), (1, 2), (2, 1), (3, 3)])
    fc_x = jnp.concatenate([x_of_rows(fc_rows), x_of_rows(out_rows)], axis=2)
    fc_sum = sum_ring(fc_x, X, x)
    out_sum = fc_sum[:, 1088:]
    h0, h1 = both(fc_sum[:, :544], fc_sum[:, 544:1088])
    h0, h1 = both(h0, swap(h1))
    fc_sum = jnp.concatenate([h0, h1], axis=1)

    g_a = tn(normed, part_a).astype(BF16).reshape(4, 4 * PIECE, 816)
    g_b = tn(normed, part_b).astype(BF16).reshape(4, 4, PIECE, 816)
    fc_sum, out_sum, proj_sum, g_a, g_b = lax.optimization_barrier((fc_sum, out_sum, proj_sum, g_a, g_b))
    g_a = sum_ring(g_a, "y", y).astype(BF16)
    g_b = sum_ring(g_b, "z", z, 1).astype(BF16)
    grad_normed = nt(jnp.concatenate([part_a, part_b], axis=1), qkv)
    grad_normed = from_order_wide(grad_normed[:128] + swap(grad_normed[128:]))
    grad_in, g_ln1_gain, g_ln1_bias = norm_back(grad_normed, first_hat, first_inverse, gain_one)
    grad_tokens = (grad_middle + grad_in).astype(BF16)

    g_hidden_bias = hidden_sum.reshape(4, 1, 544)
    zero = jnp.zeros_like(g_hidden_bias)
    g_hidden_bias = jnp.concatenate(both(g_hidden_bias, zero), axis=1).reshape(32, 136)
    sums = [
        g_ln1_gain,
        g_ln1_bias,
        columns_sum[:d],
        columns_sum[2 * d :],
        branch_sum,
        g_ln2_gain,
        g_ln2_bias,
        jnp.sum(grad_out, axis=0),
    ]
    sums = jnp.concatenate([v.reshape(32, 34) for v in sums] + [g_hidden_bias], axis=1)
    sums = sums + swap(sums)
    sums = sums + lax.ppermute(sums, "xh", SWAP)
    sums = lax.all_to_all(sums, CTX, split_axis=0, concat_axis=0, tiled=True)
    sums = jnp.sum(sums, axis=0)
    sums, g_a, g_b = lax.optimization_barrier((sums, g_a, g_b))
    g_a = sum_ring(g_a.reshape(4, PIECE, 816), "z", z).astype(BF16)
    g_b = sum_ring(g_b, "y", y).astype(BF16)
    g_qkv = jnp.stack([g_a[:34], g_a[34:68], g_b[:34], g_b[34:68]])
    qkv_sum = sum_ring(g_qkv, X, x)

    results = jnp.stack([layer_out, grad_tokens])
    first, last = results[:, :64], results[:, 64:]
    home = jnp.where(even, first, last)
    away = swap(jnp.where(even, last, first))
    placed = jnp.concatenate([jnp.where(low, home, away), jnp.where(low, away, home)], axis=1)

    v = [sums[34 * i : 34 * i + 34] for i in range(8)]
    return (
        placed[0][None],
        placed[1][None],
        v[0],
        v[1],
        qkv_sum,
        v[2],
        v[3],
        out_sum,
        v[4],
        v[5],
        v[6],
        fc_sum,
        sums[272:],
        proj_sum,
        v[7],
    )


def solution(mesh):
    grid = Mesh(mesh.devices.reshape(2, 2, 4, 2, 4), AXES)
    f = ("xh", "co")
    rows = P(f, CTX, None)
    matrix = P(CTX, f)
    vector = P(CTX)
    ins = (rows, rows, P(f), P(), vector, vector, matrix, vector, vector, matrix)
    ins = ins + (vector, vector, vector, matrix, vector, matrix, vector)
    outs = (rows, rows, vector, vector, matrix, vector, vector, matrix, vector, vector, vector)
    outs = outs + (matrix, vector, matrix, vector)
    return jax.shard_map(body, mesh=grid, in_specs=ins, out_specs=outs, check_vma=False)
```

```python
import jax
import jax.numpy as jnp
import numpy as np
from jax import lax
from jax.experimental.layout import Layout, with_layout_constraint
from jax.sharding import Mesh
from jax.sharding import PartitionSpec as P

F32 = jnp.float32
BF16 = jnp.bfloat16
HD = 64
SCALE = HD**-0.5
NEG = -1e30
AXES = ("xh", "co", "y", "xl", "z")
CTX = ("y", "xl", "z")
YZ = ("y", "z")
X = ("xh", "xl")
SWAP = [(0, 1), (1, 0)]

PIECE = 72
ORDER = np.full((16, PIECE), -1, np.int32)
for _n in range(16):
    for _xl in range(2):
        _c = (_n // 4) * 8 + _xl * 4 + _n % 4
        ORDER[_n, _xl * 34 : _xl * 34 + 34] = _c * 34 + np.arange(34)
ORDER = ORDER.reshape(-1)
DP = 16 * PIECE


def ring(n, s):
    return [(i, (i + s) % n) for i in range(n)]


def swap(v):
    return lax.ppermute(v, "co", SWAP)


def nt(a, b):
    return lax.dot_general(a, b, (((1,), (1,)), ((), ())), preferred_element_type=F32)


def nn(a, b):
    return lax.dot_general(a, b, (((1,), (0,)), ((), ())), preferred_element_type=F32)


def tn(a, b):
    return lax.dot_general(a, b, (((0,), (0,)), ((), ())), preferred_element_type=F32)


def heads(v):
    return jnp.transpose(v.reshape(2, 64, 17, 64), (0, 2, 1, 3))


def every(v):
    return jnp.broadcast_to(v[:, 16:], (2, 16, 64, 64))


def pairs_of(*parts):
    rows = [jnp.concatenate(pair, axis=3) for pair in parts]
    return jnp.concatenate(rows, axis=2).reshape(32, 64 * len(parts), 128)


def merge(first, last):
    whole = jnp.concatenate([first, last[:, None]], axis=1)
    return jnp.transpose(whole, (0, 2, 1, 3)).reshape(128, 1088)


def take(v, i):
    return lax.dynamic_index_in_dim(v, i, 0, keepdims=False)


def tile_attend(q, k, v, limit, at):
    s = jnp.where(at[:, None] <= limit[None, :], nt(k, q) * SCALE, NEG)
    top = jnp.max(s, axis=0, keepdims=True)
    e = jnp.exp(s - top)
    total = jnp.sum(e, axis=0, keepdims=True)
    out = tn(v, e.astype(BF16)) / total
    return out, top + jnp.log(total)


def tile_back(q, k, v, limit, at, g, out, lse):
    s = jnp.where(at[:, None] <= limit[None, :], nt(k, q) * SCALE, NEG)
    e = jnp.exp(s - lse)
    delta = jnp.sum(g.astype(F32).T * out, axis=0, keepdims=True)
    ds = (e * (nt(v, g) - delta)).astype(BF16)
    return tn(ds, k) * SCALE, nn(ds, q) * SCALE, nn(e.astype(BF16), g)


def rowwise(v):
    return with_layout_constraint(v, Layout(major_to_minor=(0, 1)))


def standardize(values):
    center = values - jnp.mean(values, axis=-1, keepdims=True)
    spread = jnp.mean(center * center, axis=-1, keepdims=True)
    inverse = lax.rsqrt(spread + 1e-05)
    return (center * inverse, inverse)


def norm_back(grad_result, hat, inverse, gain):
    scaled = grad_result * gain
    first = jnp.mean(scaled, axis=-1, keepdims=True)
    second = jnp.mean(scaled * hat, axis=-1, keepdims=True)
    grad_input = inverse * (scaled - first - hat * second)
    return (grad_input, jnp.sum(grad_result * hat, axis=0), jnp.sum(grad_result, axis=0))


def order_matrix():
    order = jnp.asarray(ORDER)
    return (jnp.arange(16 * 68)[:, None] == order[None, :]).astype(BF16)


def to_order(v):
    return nn(v, order_matrix()).astype(BF16)


def from_order(v):
    return nt(v, order_matrix())


def from_order_wide(v):
    high = lax.reduce_precision(v, 8, 7)
    return from_order(high.astype(BF16)) + from_order((v - high).astype(BF16))


def gather_ring(piece, axis, at):
    out = jnp.zeros((4,) + piece.shape, piece.dtype)
    out = lax.dynamic_update_index_in_dim(out, piece, at, 0)
    for s in (1, 3, 2):
        got = lax.ppermute(piece, axis, ring(4, s))
        out = lax.dynamic_update_index_in_dim(out, got, (at + 4 - s) % 4, 0)
    return out


def sum_ring(pieces, axis, at, dim=0):
    total = lax.dynamic_index_in_dim(pieces, at, dim, keepdims=False).astype(F32)
    for s in (1, 3, 2):
        part = lax.dynamic_index_in_dim(pieces, (at + s) % 4, dim, keepdims=False)
        total = total + lax.ppermute(part, axis, ring(4, s)).astype(F32)
    return total


def rows_of_x(four):
    top = jnp.concatenate([four[0], four[2]], axis=1)
    low = jnp.concatenate([four[1], four[3]], axis=1)
    return jnp.concatenate([top, low, jnp.zeros((4, top.shape[1]), top.dtype)], axis=0)


def x_of_rows(rows):
    n = rows.shape[1] // 2
    return jnp.stack([rows[:34, :n], rows[34:68, :n], rows[:34, n:], rows[34:68, n:]])


def body(
    tokens,
    cotangent,
    lengths,
    block_order,
    ln1_gain,
    ln1_bias,
    w_qkv,
    q_bias,
    v_bias,
    w_out,
    out_bias,
    ln2_gain,
    ln2_bias,
    w_fc,
    fc_bias,
    w_proj,
    proj_bias,
):
    d = 1088
    xh, co, y, xl, z = (lax.axis_index(a) for a in AXES)
    ctx = y * 8 + xl * 4 + z
    x = xh * 2 + xl
    even = co == 0

    def both(own, other):
        return jnp.where(even, own, other), jnp.where(even, other, own)

    qkv_piece = rows_of_x(gather_ring(w_qkv, X, x))
    vectors = jnp.concatenate(
        [ln1_gain, ln1_bias, q_bias, v_bias, out_bias, ln2_gain, ln2_bias, proj_bias, fc_bias]
    ).astype(F32)
    vectors, qkv_piece = lax.optimization_barrier((vectors, qkv_piece))
    vectors = lax.all_to_all(
        jnp.broadcast_to(vectors[None], (32, 408)), CTX, split_axis=0, concat_axis=0, tiled=True
    )
    qkv = lax.all_gather(qkv_piece, YZ, axis=0, tiled=True)
    w_fc, w_out, w_proj, vectors = lax.optimization_barrier((w_fc, w_out, w_proj, vectors))
    fc_keep, fc_half = both(w_fc[:, :544], w_fc[:, 544:])
    fc_own = jnp.concatenate(both(fc_keep, swap(fc_half)), axis=1)
    proj_own = lax.ppermute(w_proj, ("co", "xl"), [(0, 0), (1, 2), (2, 1), (3, 3)])
    four = gather_ring(jnp.concatenate([w_out, fc_own], axis=1), X, x)
    fc_piece = jnp.concatenate([rows_of_x(four[:, :, 272:]), rows_of_x(four[:, :, :272])], axis=1)
    four = gather_ring(proj_own, X, x)
    proj_piece = jnp.concatenate([four[0], four[1], four[2], four[3]], axis=1)
    fc_piece, proj_piece, qkv = lax.optimization_barrier((fc_piece, proj_piece, qkv))

    gain_one, bias_one, query_bias, value_bias, branch_bias, gain_two, bias_two, final_bias = (
        vectors[:, 34 * i : 34 * i + 34].reshape(1, d) for i in range(8)
    )
    hidden_bias = vectors[:, 272:].reshape(4, 2, 544)
    hidden_bias = jnp.where(even, hidden_bias[:, 0], hidden_bias[:, 1]).reshape(1, 2176)

    pair = lax.dynamic_index_in_dim(block_order, ctx, 0, keepdims=False)
    keep = (co + pair) % 2
    sent = jnp.concatenate([tokens, cotangent], axis=0)
    low = keep == 0
    kept = jnp.where(low, sent[:, :64], sent[:, 64:])
    sent = jnp.where(low, sent[:, 64:], sent[:, :64])
    slots = jnp.stack(both(kept, swap(sent)), axis=1).reshape(2, 128, d)
    length = jnp.concatenate(both(lengths, swap(lengths)))
    block = jnp.where(keep == 0, pair, 63 - pair)
    at = block * 64 + jnp.arange(64, dtype=jnp.int32)
    valid = (at[None, :] < length[:, None]).reshape(128, 1)
    mask = valid.astype(F32)

    blocks = 2 * jnp.arange(32, dtype=jnp.int32)[None, :] + jnp.arange(2, dtype=jnp.int32)[:, None]
    pairs = jnp.where(blocks < 32, blocks, 63 - blocks)
    match = pairs[:, :, None] == block_order[None, None, :]
    found = jnp.sum(jnp.where(match, jnp.arange(32, dtype=jnp.int32), 0), axis=2).astype(jnp.int32)
    own = jnp.where(even, found[0], found[1])
    oth = jnp.where(even, found[1], found[0])
    index = (block - co) // 2
    info = jnp.stack(
        [co, ctx % 16, jnp.where(index < 16, index, 31 - index), jnp.where(ctx < 16, length[0], length[1])]
    ).astype(jnp.int32)

    tokens_f = slots[0].astype(F32)
    first_hat, first_inverse = standardize(tokens_f)
    normed = to_order((first_hat * gain_one + bias_one).astype(BF16))
    normed = jnp.concatenate([normed, swap(normed)], axis=0)
    bias = jnp.concatenate([query_bias, jnp.zeros((1, d), F32), value_bias], axis=1)
    bias_a = jnp.where(even, bias[:, :816], bias[:, 816:1632])
    bias_b = jnp.where(even, bias[:, 1632:2448], bias[:, 2448:])
    projected = (nn(normed, qkv) + jnp.concatenate([bias_a, bias_b], axis=1)).astype(BF16)
    mine, theirs = projected[:128], swap(projected[128:])
    f0, f1 = both(mine[:, :816], theirs[:, :816])
    f2, f3 = both(mine[:, 816:], theirs[:, 816:])
    whole = jnp.concatenate([f0, f1, f2, f3], axis=1)
    q, k, v = (heads(whole[:, i * d : i * d + d]) for i in range(3))
    first, last = slice(0, 16), slice(16, 17)
    sent = pairs_of((q[:, first], every(q)), (k[:, first], v[:, first]), (every(v), every(k)))
    xs = lax.all_to_all(sent, CTX, split_axis=0, concat_axis=0, tiled=True)
    fc_piece, proj_piece, xs = lax.optimization_barrier((fc_piece, proj_piece, xs))
    fc_out = lax.all_gather(fc_piece, YZ, axis=0, tiled=True)
    proj = lax.all_gather(proj_piece, YZ, axis=0, tiled=True)
    fc = fc_out[:, :2176]
    out_w = fc_out[:, 2176:]
    none = jnp.zeros((DP, 272), BF16)
    o0, o1 = both(out_w[:, :272], none)
    o2, o3 = both(out_w[:, 272:], none)
    out_w = jnp.concatenate([o0, o1, o2, o3], axis=1)
    xo = swap(xs[:, 64:])
    turn = info[1]
    xs, xo = xs[own], xo[oth]
    inner = jnp.arange(64, dtype=jnp.int32)
    at_q = ((2 * jnp.arange(32, dtype=jnp.int32) + co)[:, None] * 64 + inner).reshape(2048)
    at_o = ((2 * jnp.arange(32, dtype=jnp.int32) + 1 - co)[:, None] * 64 + inner).reshape(2048)
    q_all = xs[:, :64, :64].reshape(2048, 64)
    pair_q = jnp.concatenate([take(xs, turn)[:64, 64:], take(xs, 31 - turn)[:64, 64:]], axis=0)
    k_own, v_own = xs[:, 64:128, :64].reshape(2048, 64), xs[:, 64:128, 64:].reshape(2048, 64)
    k_oth, v_oth = xo[:, :64, :64].reshape(2048, 64), xo[:, :64, 64:].reshape(2048, 64)
    v_16 = jnp.concatenate([xs[:, 128:, :64].reshape(2048, 64), xo[:, 64:, :64].reshape(2048, 64)], axis=0)
    k_16 = jnp.concatenate([xs[:, 128:, 64:].reshape(2048, 64), xo[:, 64:, 64:].reshape(2048, 64)], axis=0)
    bound = info[3] - 1
    at_all = jnp.concatenate([at_q, at_o])
    at_pair = jnp.concatenate([take(at_q.reshape(32, 64), turn), take(at_q.reshape(32, 64), 31 - turn)])
    tiles = []
    for j in range(4):
        r, n = slice(512 * j, 512 * j + 512), slice(0, 512 * j + 512)
        keys = jnp.concatenate([k_own[n], k_oth[n]], axis=0)
        values = jnp.concatenate([v_own[n], v_oth[n]], axis=0)
        at = jnp.concatenate([at_q[n], at_o[n]])
        limit = jnp.minimum(at_q[r], bound)
        tiles.append((r, n, keys, values, limit, at, q_all[r]))
    outs = [tile_attend(q, keys, values, limit, at) for r, n, keys, values, limit, at, q in tiles]
    pair_limit = jnp.minimum(at_pair, bound)
    out_16, lse_16 = tile_attend(pair_q, k_16, v_16, pair_limit, at_all)
    inverse = jnp.sum(jnp.where(own[None, :] == jnp.arange(32)[:, None], jnp.arange(32), 0), axis=1)
    is_turn = jnp.arange(32)[:, None, None]
    low_16 = out_16.T.reshape(2, 64, 64)
    wide = jnp.where(is_turn == turn, low_16[0], jnp.where(is_turn == 31 - turn, low_16[1], 0.0))
    low_all = jnp.concatenate([o.T for o, _ in outs], axis=0).reshape(32, 64, 64)
    o_sent = jnp.concatenate([wide, low_all], axis=2).astype(BF16)[inverse]
    o_got = lax.all_to_all(o_sent, CTX, split_axis=0, concat_axis=0, tiled=True)
    o_got = o_got.reshape(2, 16, 64, 128)
    home_turn = info[2]

    def turned(v):
        return lax.dynamic_index_in_dim(v, home_turn, 1, keepdims=False)

    attended = to_order(merge(o_got[..., 64:], turned(o_got[..., :64])))
    attended = jnp.concatenate([attended, swap(attended)], axis=0)
    branch = nn(attended, out_w)
    middle = tokens_f + (branch[:128] + swap(branch[128:])) + branch_bias
    second_hat, second_inverse = standardize(middle)
    second = to_order((second_hat * gain_two + bias_two).astype(BF16))
    second = jnp.concatenate([second, swap(second)], axis=0)
    hidden = nn(second, fc) + hidden_bias
    active, gelu_pull = jax.vjp(lambda h: jax.nn.gelu(h, approximate=True), hidden)
    active = lax.reduce_precision(active, 8, 7).astype(BF16)
    final = nn(active, proj)
    final = final[:128] + swap(final[128:]) + final_bias
    layer_out = (mask * (middle + final)).astype(BF16)

    grad_out_low = jnp.where(valid, slots[1], BF16(0))
    grad_out = grad_out_low.astype(F32)
    grad_out_two = jnp.concatenate([grad_out_low, swap(grad_out_low)], axis=0)
    (grad_hidden,) = gelu_pull(nt(grad_out_two, proj))
    grad_hidden = lax.reduce_precision(grad_hidden, 8, 7)
    hidden_sum = jnp.sum(grad_hidden, axis=0)
    grad_hidden = grad_hidden.astype(BF16)
    grad_second = nt(grad_hidden, fc)
    grad_second = from_order_wide(grad_second[:128] + swap(grad_second[128:]))
    grad_mid, g_ln2_gain, g_ln2_bias = norm_back(grad_second, second_hat, second_inverse, gain_two)
    grad_middle = grad_out + grad_mid
    grad_branch = lax.reduce_precision(grad_middle, 8, 7)
    branch_sum = jnp.sum(grad_branch, axis=0)
    grad_branch = grad_branch.astype(BF16)
    whole_branch = both_branch = jnp.concatenate([grad_branch, swap(grad_branch)], axis=0)
    both_branch = jnp.concatenate(
        [
            jnp.where(even, both_branch[:, :272], both_branch[:, 272:544]),
            jnp.where(even, both_branch[:, 544:816], both_branch[:, 816:]),
        ],
        axis=1,
    )
    grad_attn = nt(whole_branch, out_w)
    grad_attn = (grad_attn[:128] + swap(grad_attn[128:])).astype(BF16)
    grad_attn = from_order(grad_attn).astype(BF16)
    g = heads(grad_attn)
    sent = pairs_of((every(g), g[:, first]))
    sent, active, grad_out_two, second, grad_hidden, attended, both_branch = lax.optimization_barrier(
        (sent, active, grad_out_two, second, grad_hidden, attended, both_branch)
    )
    ga = lax.all_to_all(sent, CTX, split_axis=0, concat_axis=0, tiled=True)
    g_proj = rowwise(tn(active, grad_out_two).astype(BF16)).reshape(16, 136, d)
    g_fc = [rowwise(tn(second, grad_hidden[:, i * d : i * d + d]).astype(BF16)).reshape(16, PIECE, d) for i in range(2)]
    g_out = jnp.pad(rowwise(tn(attended, both_branch).astype(BF16)).reshape(16, PIECE, 544), ((0, 0), (0, 0), (0, 544)))
    packed = jnp.concatenate(g_fc + [g_out, g_proj], axis=1)
    packed = lax.psum_scatter(packed.reshape(16 * 352, d), YZ, scatter_dimension=0, tiled=True)
    packed = lax.optimization_barrier(packed)
    ga = ga[own]
    g_all = ga[:, :, 64:].reshape(2048, 64)
    pair_g = jnp.concatenate([take(ga, turn)[:, :64], take(ga, 31 - turn)[:, :64]], axis=0)
    dqs = []
    dk = [jnp.zeros((2048, 64), F32), jnp.zeros((2048, 64), F32)]
    dv = [jnp.zeros((2048, 64), F32), jnp.zeros((2048, 64), F32)]
    for (r, n, keys, values, limit, at, q), (out, lse) in zip(tiles, outs):
        dq, dk_part, dv_part = tile_back(q, keys, values, limit, at, g_all[r], out, lse)
        dqs.append(dq)
        rows = n.stop
        for i in range(2):
            grow = ((0, 2048 - rows), (0, 0))
            dk[i] = dk[i] + jnp.pad(dk_part[i * rows : i * rows + rows], grow)
            dv[i] = dv[i] + jnp.pad(dv_part[i * rows : i * rows + rows], grow)
    dq_16, dk_16, dv_16 = tile_back(pair_q, k_16, v_16, pair_limit, at_all, pair_g, out_16, lse_16)
    dq_16 = dq_16.reshape(2, 64, 64)
    wide = jnp.where(is_turn == turn, dq_16[0], jnp.where(is_turn == 31 - turn, dq_16[1], 0.0))
    dq = jnp.concatenate([jnp.concatenate(dqs, axis=0).reshape(32, 64, 64), wide], axis=2).astype(BF16)
    mine = jnp.concatenate([dk[0], dv[0], dv_16[:2048], dk_16[:2048]], axis=1)
    theirs = jnp.concatenate([dk[1], dv[1], dv_16[2048:], dk_16[2048:]], axis=1).astype(BF16)
    total = (mine + swap(theirs).astype(F32)).astype(BF16).reshape(32, 64, 256)
    sent = jnp.concatenate([dq, total[:, :, :128], total[:, :, 128:]], axis=1)[inverse]
    got = lax.all_to_all(sent, CTX, split_axis=0, concat_axis=0, tiled=True)
    got = got.reshape(2, 16, 192, 128)
    last = jnp.sum(got[:, :, 128:].astype(F32), axis=1).astype(BF16)
    grad_projected = jnp.concatenate(
        [
            merge(got[:, :, :64, :64], turned(got[:, :, :64, 64:])),
            merge(got[:, :, 64:128, :64], last[:, :, 64:]),
            merge(got[:, :, 64:128, 64:], last[:, :, :64]),
        ],
        axis=1,
    )
    columns_sum = jnp.sum(grad_projected.astype(F32), axis=0)
    f0, f1 = both(grad_projected[:, :816], grad_projected[:, 816:1632])
    f2, f3 = both(grad_projected[:, 1632:2448], grad_projected[:, 2448:])
    part_a = jnp.concatenate([f0, swap(f1)], axis=0)
    part_b = jnp.concatenate([f2, swap(f3)], axis=0)
    fc_rows = jnp.concatenate([packed[:PIECE], packed[PIECE : 2 * PIECE]], axis=1)
    out_rows = packed[2 * PIECE : 3 * PIECE, :544]
    proj_rows = packed[3 * PIECE :]
    proj_x = jnp.stack([proj_rows[:, i * 272 : i * 272 + 272] for i in range(4)])
    proj_sum = sum_ring(proj_x, X, x)
    proj_sum = lax.ppermute(proj_sum, ("co", "xl"), [(0, 0), (1, 2), (2, 1), (3, 3)])
    fc_x = jnp.concatenate([x_of_rows(fc_rows), x_of_rows(out_rows)], axis=2)
    fc_sum = sum_ring(fc_x, X, x)
    out_sum = fc_sum[:, 1088:]
    h0, h1 = both(fc_sum[:, :544], fc_sum[:, 544:1088])
    h0, h1 = both(h0, swap(h1))
    fc_sum = jnp.concatenate([h0, h1], axis=1)

    g_a = rowwise(tn(normed, part_a).astype(BF16)).reshape(4, 4 * PIECE, 816)
    g_b = rowwise(tn(normed, part_b).astype(BF16)).reshape(4, 4, PIECE, 816)
    fc_sum, out_sum, proj_sum, g_a, g_b = lax.optimization_barrier((fc_sum, out_sum, proj_sum, g_a, g_b))
    g_a = sum_ring(g_a, "y", y).astype(BF16)
    g_b = sum_ring(g_b, "z", z, 1).astype(BF16)
    grad_normed = nt(jnp.concatenate([part_a, part_b], axis=1), qkv)
    grad_normed = from_order_wide(grad_normed[:128] + swap(grad_normed[128:]))
    grad_in, g_ln1_gain, g_ln1_bias = norm_back(grad_normed, first_hat, first_inverse, gain_one)
    grad_tokens = (grad_middle + grad_in).astype(BF16)

    g_hidden_bias = hidden_sum.reshape(4, 1, 544)
    zero = jnp.zeros_like(g_hidden_bias)
    g_hidden_bias = jnp.concatenate(both(g_hidden_bias, zero), axis=1).reshape(32, 136)
    sums = [
        g_ln1_gain,
        g_ln1_bias,
        columns_sum[:d],
        columns_sum[2 * d :],
        branch_sum,
        g_ln2_gain,
        g_ln2_bias,
        jnp.sum(grad_out, axis=0),
    ]
    sums = jnp.concatenate([v.reshape(32, 34) for v in sums] + [g_hidden_bias], axis=1)
    sums = sums + swap(sums)
    sums = sums + lax.ppermute(sums, "xh", SWAP)
    sums = lax.all_to_all(sums, CTX, split_axis=0, concat_axis=0, tiled=True)
    sums = jnp.sum(sums, axis=0)
    sums, g_a, g_b = lax.optimization_barrier((sums, g_a, g_b))
    g_a = sum_ring(g_a.reshape(4, PIECE, 816), "z", z).astype(BF16)
    g_b = sum_ring(g_b, "y", y).astype(BF16)
    g_qkv = jnp.stack([g_a[:34], g_a[34:68], g_b[:34], g_b[34:68]])
    qkv_sum = sum_ring(g_qkv, X, x)

    results = jnp.stack([layer_out, grad_tokens])
    first, last = results[:, :64], results[:, 64:]
    home = jnp.where(even, first, last)
    away = swap(jnp.where(even, last, first))
    placed = jnp.concatenate([jnp.where(low, home, away), jnp.where(low, away, home)], axis=1)

    v = [sums[34 * i : 34 * i + 34] for i in range(8)]
    return (
        placed[0][None],
        placed[1][None],
        v[0],
        v[1],
        qkv_sum,
        v[2],
        v[3],
        out_sum,
        v[4],
        v[5],
        v[6],
        fc_sum,
        sums[272:],
        proj_sum,
        v[7],
    )


def solution(mesh):
    grid = Mesh(mesh.devices.reshape(2, 2, 4, 2, 4), AXES)
    f = ("xh", "co")
    rows = P(f, CTX, None)
    matrix = P(CTX, f)
    vector = P(CTX)
    ins = (rows, rows, P(f), P(), vector, vector, matrix, vector, vector, matrix)
    ins = ins + (vector, vector, vector, matrix, vector, matrix, vector)
    outs = (rows, rows, vector, vector, matrix, vector, vector, matrix, vector, vector, vector)
    outs = outs + (matrix, vector, matrix, vector)
    return jax.shard_map(body, mesh=grid, in_specs=ins, out_specs=outs, check_vma=False)
```

```python
import jax
import jax.numpy as jnp
import numpy as np
from jax import lax
from jax.experimental.layout import Layout, with_layout_constraint
from jax.sharding import Mesh
from jax.sharding import PartitionSpec as P

F32 = jnp.float32
BF16 = jnp.bfloat16
HD = 64
SCALE = HD**-0.5
NEG = -1e30
AXES = ("xh", "co", "y", "xl", "z")
CTX = ("y", "xl", "z")
YZ = ("y", "z")
X = ("xh", "xl")
SWAP = [(0, 1), (1, 0)]

PIECE = 72
ORDER = np.full((16, PIECE), -1, np.int32)
for _n in range(16):
    for _xl in range(2):
        _c = (_n // 4) * 8 + _xl * 4 + _n % 4
        ORDER[_n, _xl * 34 : _xl * 34 + 34] = _c * 34 + np.arange(34)
ORDER = ORDER.reshape(-1)
DP = 16 * PIECE


def ring(n, s):
    return [(i, (i + s) % n) for i in range(n)]


def swap(v):
    return lax.ppermute(v, "co", SWAP)


def nt(a, b):
    return lax.dot_general(a, b, (((1,), (1,)), ((), ())), preferred_element_type=F32)


def nn(a, b):
    return lax.dot_general(a, b, (((1,), (0,)), ((), ())), preferred_element_type=F32)


def tn(a, b):
    return lax.dot_general(a, b, (((0,), (0,)), ((), ())), preferred_element_type=F32)


def heads(v):
    return jnp.transpose(v.reshape(2, 64, 17, 64), (0, 2, 1, 3))


def every(v):
    return jnp.broadcast_to(v[:, 16:], (2, 16, 64, 64))


def pairs_of(*parts):
    rows = [jnp.concatenate(pair, axis=3) for pair in parts]
    return jnp.concatenate(rows, axis=2).reshape(32, 64 * len(parts), 128)


def merge(first, last):
    whole = jnp.concatenate([first, last[:, None]], axis=1)
    return jnp.transpose(whole, (0, 2, 1, 3)).reshape(128, 1088)


def take(v, i):
    return lax.dynamic_index_in_dim(v, i, 0, keepdims=False)


def tile_attend(q, k, v, limit, at):
    s = jnp.where(at[:, None] <= limit[None, :], nt(k, q) * SCALE, NEG)
    top = jnp.max(s, axis=0, keepdims=True)
    e = jnp.exp(s - top)
    total = jnp.sum(e, axis=0, keepdims=True)
    out = tn(v, e.astype(BF16)) / total
    return out, top + jnp.log(total)


def tile_back(q, k, v, limit, at, g, out, lse):
    s = jnp.where(at[:, None] <= limit[None, :], nt(k, q) * SCALE, NEG)
    e = jnp.exp(s - lse)
    delta = jnp.sum(g.astype(F32).T * out, axis=0, keepdims=True)
    ds = (e * (nt(v, g) - delta)).astype(BF16)
    return tn(ds, k) * SCALE, nn(ds, q) * SCALE, nn(e.astype(BF16), g)


def rowwise(v):
    return with_layout_constraint(v, Layout(major_to_minor=(0, 1)))


def standardize(values):
    center = values - jnp.mean(values, axis=-1, keepdims=True)
    spread = jnp.mean(center * center, axis=-1, keepdims=True)
    inverse = lax.rsqrt(spread + 1e-05)
    return (center * inverse, inverse)


def norm_back(grad_result, hat, inverse, gain):
    scaled = grad_result * gain
    first = jnp.mean(scaled, axis=-1, keepdims=True)
    second = jnp.mean(scaled * hat, axis=-1, keepdims=True)
    grad_input = inverse * (scaled - first - hat * second)
    return (grad_input, jnp.sum(grad_result * hat, axis=0), jnp.sum(grad_result, axis=0))


def order_matrix():
    order = jnp.asarray(ORDER)
    return (jnp.arange(16 * 68)[:, None] == order[None, :]).astype(BF16)


def to_order(v):
    return nn(v, order_matrix()).astype(BF16)


def from_order(v):
    return nt(v, order_matrix())


def from_order_wide(v):
    high = lax.reduce_precision(v, 8, 7)
    return from_order(high.astype(BF16)) + from_order((v - high).astype(BF16))


def gather_ring(piece, axis, at):
    out = jnp.zeros((4,) + piece.shape, piece.dtype)
    out = lax.dynamic_update_index_in_dim(out, piece, at, 0)
    for s in (1, 3, 2):
        got = lax.ppermute(piece, axis, ring(4, s))
        out = lax.dynamic_update_index_in_dim(out, got, (at + 4 - s) % 4, 0)
    return out


def sum_ring(pieces, axis, at, dim=0):
    total = lax.dynamic_index_in_dim(pieces, at, dim, keepdims=False).astype(F32)
    for s in (1, 3, 2):
        part = lax.dynamic_index_in_dim(pieces, (at + s) % 4, dim, keepdims=False)
        total = total + lax.ppermute(part, axis, ring(4, s)).astype(F32)
    return total


def rows_of_x(four):
    top = jnp.concatenate([four[0], four[2]], axis=1)
    low = jnp.concatenate([four[1], four[3]], axis=1)
    return jnp.concatenate([top, low, jnp.zeros((4, top.shape[1]), top.dtype)], axis=0)


def x_of_rows(rows):
    n = rows.shape[1] // 2
    return jnp.stack([rows[:34, :n], rows[34:68, :n], rows[:34, n:], rows[34:68, n:]])


def body(
    tokens,
    cotangent,
    lengths,
    block_order,
    ln1_gain,
    ln1_bias,
    w_qkv,
    q_bias,
    v_bias,
    w_out,
    out_bias,
    ln2_gain,
    ln2_bias,
    w_fc,
    fc_bias,
    w_proj,
    proj_bias,
):
    d = 1088
    xh, co, y, xl, z = (lax.axis_index(a) for a in AXES)
    ctx = y * 8 + xl * 4 + z
    x = xh * 2 + xl
    even = co == 0

    def both(own, other):
        return jnp.where(even, own, other), jnp.where(even, other, own)

    qkv_piece = rows_of_x(gather_ring(w_qkv, X, x))
    vectors = jnp.concatenate(
        [ln1_gain, ln1_bias, q_bias, v_bias, out_bias, ln2_gain, ln2_bias, proj_bias, fc_bias]
    ).astype(F32)
    vectors, qkv_piece = lax.optimization_barrier((vectors, qkv_piece))
    vectors = lax.all_to_all(
        jnp.broadcast_to(vectors[None], (32, 408)), CTX, split_axis=0, concat_axis=0, tiled=True
    )
    qkv = lax.all_gather(qkv_piece, YZ, axis=0, tiled=True)
    w_fc, w_out, w_proj, vectors = lax.optimization_barrier((w_fc, w_out, w_proj, vectors))
    fc_keep, fc_half = both(w_fc[:, :544], w_fc[:, 544:])
    fc_own = jnp.concatenate(both(fc_keep, swap(fc_half)), axis=1)
    proj_own = lax.ppermute(w_proj, ("co", "xl"), [(0, 0), (1, 2), (2, 1), (3, 3)])
    four = gather_ring(jnp.concatenate([w_out, fc_own], axis=1), X, x)
    out_piece = rows_of_x(four[:, :, :272])
    none = jnp.zeros((PIECE, 272), BF16)
    o0, o1 = both(out_piece[:, :272], none)
    o2, o3 = both(out_piece[:, 272:], none)
    fc_piece = jnp.concatenate([rows_of_x(four[:, :, 272:]), o0, o1, o2, o3], axis=1)
    four = gather_ring(proj_own, X, x)
    proj_piece = jnp.concatenate([four[0], four[1], four[2], four[3]], axis=1)
    fc_piece, proj_piece, qkv = lax.optimization_barrier((fc_piece, proj_piece, qkv))
    fc_out = lax.all_gather(fc_piece, YZ, axis=0, tiled=True)
    proj = lax.all_gather(proj_piece, YZ, axis=0, tiled=True)
    fc = fc_out[:, :2176]
    out_w = fc_out[:, 2176:]

    gain_one, bias_one, query_bias, value_bias, branch_bias, gain_two, bias_two, final_bias = (
        vectors[:, 34 * i : 34 * i + 34].reshape(1, d) for i in range(8)
    )
    hidden_bias = vectors[:, 272:].reshape(4, 2, 544)
    hidden_bias = jnp.where(even, hidden_bias[:, 0], hidden_bias[:, 1]).reshape(1, 2176)

    pair = lax.dynamic_index_in_dim(block_order, ctx, 0, keepdims=False)
    keep = (co + pair) % 2
    sent = jnp.concatenate([tokens, cotangent], axis=0)
    low = keep == 0
    kept = jnp.where(low, sent[:, :64], sent[:, 64:])
    sent = jnp.where(low, sent[:, 64:], sent[:, :64])
    slots = jnp.stack(both(kept, swap(sent)), axis=1).reshape(2, 128, d)
    length = jnp.concatenate(both(lengths, swap(lengths)))
    block = jnp.where(keep == 0, pair, 63 - pair)
    at = block * 64 + jnp.arange(64, dtype=jnp.int32)
    valid = (at[None, :] < length[:, None]).reshape(128, 1)
    mask = valid.astype(F32)

    blocks = 2 * jnp.arange(32, dtype=jnp.int32)[None, :] + jnp.arange(2, dtype=jnp.int32)[:, None]
    pairs = jnp.where(blocks < 32, blocks, 63 - blocks)
    match = pairs[:, :, None] == block_order[None, None, :]
    found = jnp.sum(jnp.where(match, jnp.arange(32, dtype=jnp.int32), 0), axis=2).astype(jnp.int32)
    own = jnp.where(even, found[0], found[1])
    oth = jnp.where(even, found[1], found[0])
    index = (block - co) // 2
    info = jnp.stack(
        [co, ctx % 16, jnp.where(index < 16, index, 31 - index), jnp.where(ctx < 16, length[0], length[1])]
    ).astype(jnp.int32)

    tokens_f = slots[0].astype(F32)
    first_hat, first_inverse = standardize(tokens_f)
    normed = to_order((first_hat * gain_one + bias_one).astype(BF16))
    normed = jnp.concatenate([normed, swap(normed)], axis=0)
    bias = jnp.concatenate([query_bias, jnp.zeros((1, d), F32), value_bias], axis=1)
    bias_a = jnp.where(even, bias[:, :816], bias[:, 816:1632])
    bias_b = jnp.where(even, bias[:, 1632:2448], bias[:, 2448:])
    projected = (nn(normed, qkv) + jnp.concatenate([bias_a, bias_b], axis=1)).astype(BF16)
    mine, theirs = projected[:128], swap(projected[128:])
    f0, f1 = both(mine[:, :816], theirs[:, :816])
    f2, f3 = both(mine[:, 816:], theirs[:, 816:])
    whole = jnp.concatenate([f0, f1, f2, f3], axis=1)
    q, k, v = (heads(whole[:, i * d : i * d + d]) for i in range(3))
    first, last = slice(0, 16), slice(16, 17)
    sent = pairs_of((q[:, first], every(q)), (k[:, first], v[:, first]), (every(v), every(k)))
    xs = lax.all_to_all(sent, CTX, split_axis=0, concat_axis=0, tiled=True)
    xo = swap(xs[:, 64:])
    turn = info[1]
    xs, xo = xs[own], xo[oth]
    inner = jnp.arange(64, dtype=jnp.int32)
    at_q = ((2 * jnp.arange(32, dtype=jnp.int32) + co)[:, None] * 64 + inner).reshape(2048)
    at_o = ((2 * jnp.arange(32, dtype=jnp.int32) + 1 - co)[:, None] * 64 + inner).reshape(2048)
    q_all = xs[:, :64, :64].reshape(2048, 64)
    pair_q = jnp.concatenate([take(xs, turn)[:64, 64:], take(xs, 31 - turn)[:64, 64:]], axis=0)
    k_own, v_own = xs[:, 64:128, :64].reshape(2048, 64), xs[:, 64:128, 64:].reshape(2048, 64)
    k_oth, v_oth = xo[:, :64, :64].reshape(2048, 64), xo[:, :64, 64:].reshape(2048, 64)
    v_16 = jnp.concatenate([xs[:, 128:, :64].reshape(2048, 64), xo[:, 64:, :64].reshape(2048, 64)], axis=0)
    k_16 = jnp.concatenate([xs[:, 128:, 64:].reshape(2048, 64), xo[:, 64:, 64:].reshape(2048, 64)], axis=0)
    bound = info[3] - 1
    at_all = jnp.concatenate([at_q, at_o])
    at_pair = jnp.concatenate([take(at_q.reshape(32, 64), turn), take(at_q.reshape(32, 64), 31 - turn)])
    tiles = []
    for j in range(4):
        r, n = slice(512 * j, 512 * j + 512), slice(0, 512 * j + 512)
        keys = jnp.concatenate([k_own[n], k_oth[n]], axis=0)
        values = jnp.concatenate([v_own[n], v_oth[n]], axis=0)
        at = jnp.concatenate([at_q[n], at_o[n]])
        limit = jnp.minimum(at_q[r], bound)
        tiles.append((r, n, keys, values, limit, at, q_all[r]))
    outs = [tile_attend(q, keys, values, limit, at) for r, n, keys, values, limit, at, q in tiles]
    pair_limit = jnp.minimum(at_pair, bound)
    out_16, lse_16 = tile_attend(pair_q, k_16, v_16, pair_limit, at_all)
    inverse = jnp.sum(jnp.where(own[None, :] == jnp.arange(32)[:, None], jnp.arange(32), 0), axis=1)
    is_turn = jnp.arange(32)[:, None, None]
    low_16 = out_16.T.reshape(2, 64, 64)
    wide = jnp.where(is_turn == turn, low_16[0], jnp.where(is_turn == 31 - turn, low_16[1], 0.0))
    low_all = jnp.concatenate([o.T for o, _ in outs], axis=0).reshape(32, 64, 64)
    o_sent = jnp.concatenate([wide, low_all], axis=2).astype(BF16)[inverse]
    o_got = lax.all_to_all(o_sent, CTX, split_axis=0, concat_axis=0, tiled=True)
    o_got = o_got.reshape(2, 16, 64, 128)
    home_turn = info[2]

    def turned(v):
        return lax.dynamic_index_in_dim(v, home_turn, 1, keepdims=False)

    attended = to_order(merge(o_got[..., 64:], turned(o_got[..., :64])))
    attended = jnp.concatenate([attended, swap(attended)], axis=0)
    branch = nn(attended, out_w)
    middle = tokens_f + (branch[:128] + swap(branch[128:])) + branch_bias
    second_hat, second_inverse = standardize(middle)
    second = to_order((second_hat * gain_two + bias_two).astype(BF16))
    second = jnp.concatenate([second, swap(second)], axis=0)
    hidden = nn(second, fc) + hidden_bias
    active, gelu_pull = jax.vjp(lambda h: jax.nn.gelu(h, approximate=True), hidden)
    active = lax.reduce_precision(active, 8, 7).astype(BF16)
    final = nn(active, proj)
    final = final[:128] + swap(final[128:]) + final_bias
    layer_out = (mask * (middle + final)).astype(BF16)

    grad_out_low = jnp.where(valid, slots[1], BF16(0))
    grad_out = grad_out_low.astype(F32)
    grad_out_two = jnp.concatenate([grad_out_low, swap(grad_out_low)], axis=0)
    (grad_hidden,) = gelu_pull(nt(grad_out_two, proj))
    grad_hidden = lax.reduce_precision(grad_hidden, 8, 7)
    hidden_sum = jnp.sum(grad_hidden, axis=0)
    grad_hidden = grad_hidden.astype(BF16)
    grad_second = nt(grad_hidden, fc)
    grad_second = from_order_wide(grad_second[:128] + swap(grad_second[128:]))
    grad_mid, g_ln2_gain, g_ln2_bias = norm_back(grad_second, second_hat, second_inverse, gain_two)
    grad_middle = grad_out + grad_mid
    grad_branch = lax.reduce_precision(grad_middle, 8, 7)
    branch_sum = jnp.sum(grad_branch, axis=0)
    grad_branch = grad_branch.astype(BF16)
    whole_branch = both_branch = jnp.concatenate([grad_branch, swap(grad_branch)], axis=0)
    both_branch = jnp.concatenate(
        [
            jnp.where(even, both_branch[:, :272], both_branch[:, 272:544]),
            jnp.where(even, both_branch[:, 544:816], both_branch[:, 816:]),
        ],
        axis=1,
    )
    grad_attn = nt(whole_branch, out_w)
    grad_attn = (grad_attn[:128] + swap(grad_attn[128:])).astype(BF16)
    grad_attn = from_order(grad_attn).astype(BF16)
    g = heads(grad_attn)
    sent = pairs_of((every(g), g[:, first]))
    sent, active, grad_out_two, second, grad_hidden, attended, both_branch = lax.optimization_barrier(
        (sent, active, grad_out_two, second, grad_hidden, attended, both_branch)
    )
    ga = lax.all_to_all(sent, CTX, split_axis=0, concat_axis=0, tiled=True)
    g_proj = rowwise(tn(active, grad_out_two).astype(BF16)).reshape(16, 136, d)
    g_fc = [rowwise(tn(second, grad_hidden[:, i * d : i * d + d]).astype(BF16)).reshape(16, PIECE, d) for i in range(2)]
    g_out = jnp.pad(rowwise(tn(attended, both_branch).astype(BF16)).reshape(16, PIECE, 544), ((0, 0), (0, 0), (0, 544)))
    packed = jnp.concatenate(g_fc + [g_out, g_proj], axis=1)
    packed = lax.psum_scatter(packed.reshape(16 * 352, d), YZ, scatter_dimension=0, tiled=True)
    packed = lax.optimization_barrier(packed)
    ga = ga[own]
    g_all = ga[:, :, 64:].reshape(2048, 64)
    pair_g = jnp.concatenate([take(ga, turn)[:, :64], take(ga, 31 - turn)[:, :64]], axis=0)
    dqs = []
    dk = [jnp.zeros((2048, 64), F32), jnp.zeros((2048, 64), F32)]
    dv = [jnp.zeros((2048, 64), F32), jnp.zeros((2048, 64), F32)]
    for (r, n, keys, values, limit, at, q), (out, lse) in zip(tiles, outs):
        dq, dk_part, dv_part = tile_back(q, keys, values, limit, at, g_all[r], out, lse)
        dqs.append(dq)
        rows = n.stop
        for i in range(2):
            grow = ((0, 2048 - rows), (0, 0))
            dk[i] = dk[i] + jnp.pad(dk_part[i * rows : i * rows + rows], grow)
            dv[i] = dv[i] + jnp.pad(dv_part[i * rows : i * rows + rows], grow)
    dq_16, dk_16, dv_16 = tile_back(pair_q, k_16, v_16, pair_limit, at_all, pair_g, out_16, lse_16)
    dq_16 = dq_16.reshape(2, 64, 64)
    wide = jnp.where(is_turn == turn, dq_16[0], jnp.where(is_turn == 31 - turn, dq_16[1], 0.0))
    dq = jnp.concatenate([jnp.concatenate(dqs, axis=0).reshape(32, 64, 64), wide], axis=2).astype(BF16)
    mine = jnp.concatenate([dk[0], dv[0], dv_16[:2048], dk_16[:2048]], axis=1)
    theirs = jnp.concatenate([dk[1], dv[1], dv_16[2048:], dk_16[2048:]], axis=1).astype(BF16)
    total = (mine + swap(theirs).astype(F32)).astype(BF16).reshape(32, 64, 256)
    sent = jnp.concatenate([dq, total[:, :, :128], total[:, :, 128:]], axis=1)[inverse]
    got = lax.all_to_all(sent, CTX, split_axis=0, concat_axis=0, tiled=True)
    got = got.reshape(2, 16, 192, 128)
    last = jnp.sum(got[:, :, 128:].astype(F32), axis=1).astype(BF16)
    grad_projected = jnp.concatenate(
        [
            merge(got[:, :, :64, :64], turned(got[:, :, :64, 64:])),
            merge(got[:, :, 64:128, :64], last[:, :, 64:]),
            merge(got[:, :, 64:128, 64:], last[:, :, :64]),
        ],
        axis=1,
    )
    columns_sum = jnp.sum(grad_projected.astype(F32), axis=0)
    f0, f1 = both(grad_projected[:, :816], grad_projected[:, 816:1632])
    f2, f3 = both(grad_projected[:, 1632:2448], grad_projected[:, 2448:])
    part_a = jnp.concatenate([f0, swap(f1)], axis=0)
    part_b = jnp.concatenate([f2, swap(f3)], axis=0)
    fc_rows = jnp.concatenate([packed[:PIECE], packed[PIECE : 2 * PIECE]], axis=1)
    out_rows = packed[2 * PIECE : 3 * PIECE, :544]
    proj_rows = packed[3 * PIECE :]
    proj_x = jnp.stack([proj_rows[:, i * 272 : i * 272 + 272] for i in range(4)])
    proj_sum = sum_ring(proj_x, X, x)
    proj_sum = lax.ppermute(proj_sum, ("co", "xl"), [(0, 0), (1, 2), (2, 1), (3, 3)])
    fc_x = jnp.concatenate([x_of_rows(fc_rows), x_of_rows(out_rows)], axis=2)
    fc_sum = sum_ring(fc_x, X, x)
    out_sum = fc_sum[:, 1088:]
    h0, h1 = both(fc_sum[:, :544], fc_sum[:, 544:1088])
    h0, h1 = both(h0, swap(h1))
    fc_sum = jnp.concatenate([h0, h1], axis=1)

    g_a = rowwise(tn(normed, part_a).astype(BF16)).reshape(4, 4 * PIECE, 816)
    g_b = rowwise(tn(normed, part_b).astype(BF16)).reshape(4, 4, PIECE, 816)
    fc_sum, out_sum, proj_sum, g_a, g_b = lax.optimization_barrier((fc_sum, out_sum, proj_sum, g_a, g_b))
    g_a = sum_ring(g_a, "y", y).astype(BF16)
    g_b = sum_ring(g_b, "z", z, 1).astype(BF16)
    grad_normed = nt(jnp.concatenate([part_a, part_b], axis=1), qkv)
    grad_normed = from_order_wide(grad_normed[:128] + swap(grad_normed[128:]))
    grad_in, g_ln1_gain, g_ln1_bias = norm_back(grad_normed, first_hat, first_inverse, gain_one)
    grad_tokens = (grad_middle + grad_in).astype(BF16)

    g_hidden_bias = hidden_sum.reshape(4, 1, 544)
    zero = jnp.zeros_like(g_hidden_bias)
    g_hidden_bias = jnp.concatenate(both(g_hidden_bias, zero), axis=1).reshape(32, 136)
    sums = [
        g_ln1_gain,
        g_ln1_bias,
        columns_sum[:d],
        columns_sum[2 * d :],
        branch_sum,
        g_ln2_gain,
        g_ln2_bias,
        jnp.sum(grad_out, axis=0),
    ]
    sums = jnp.concatenate([v.reshape(32, 34) for v in sums] + [g_hidden_bias], axis=1)
    sums = sums + swap(sums)
    sums = sums + lax.ppermute(sums, "xh", SWAP)
    sums = lax.all_to_all(sums, CTX, split_axis=0, concat_axis=0, tiled=True)
    sums = jnp.sum(sums, axis=0)
    sums, g_a, g_b = lax.optimization_barrier((sums, g_a, g_b))
    g_a = sum_ring(g_a.reshape(4, PIECE, 816), "z", z).astype(BF16)
    g_b = sum_ring(g_b, "y", y).astype(BF16)
    g_qkv = jnp.stack([g_a[:34], g_a[34:68], g_b[:34], g_b[34:68]])
    qkv_sum = sum_ring(g_qkv, X, x)

    results = jnp.stack([layer_out, grad_tokens])
    first, last = results[:, :64], results[:, 64:]
    home = jnp.where(even, first, last)
    away = swap(jnp.where(even, last, first))
    placed = jnp.concatenate([jnp.where(low, home, away), jnp.where(low, away, home)], axis=1)

    v = [sums[34 * i : 34 * i + 34] for i in range(8)]
    return (
        placed[0][None],
        placed[1][None],
        v[0],
        v[1],
        qkv_sum,
        v[2],
        v[3],
        out_sum,
        v[4],
        v[5],
        v[6],
        fc_sum,
        sums[272:],
        proj_sum,
        v[7],
    )


def solution(mesh):
    grid = Mesh(mesh.devices.reshape(2, 2, 4, 2, 4), AXES)
    f = ("xh", "co")
    rows = P(f, CTX, None)
    matrix = P(CTX, f)
    vector = P(CTX)
    ins = (rows, rows, P(f), P(), vector, vector, matrix, vector, vector, matrix)
    ins = ins + (vector, vector, vector, matrix, vector, matrix, vector)
    outs = (rows, rows, vector, vector, matrix, vector, vector, matrix, vector, vector, vector)
    outs = outs + (matrix, vector, matrix, vector)
    return jax.shard_map(body, mesh=grid, in_specs=ins, out_specs=outs, check_vma=False)
```

```python
import jax
import jax.numpy as jnp
import numpy as np
from jax import lax
from jax.experimental.layout import Layout, with_layout_constraint
from jax.sharding import Mesh
from jax.sharding import PartitionSpec as P

F32 = jnp.float32
BF16 = jnp.bfloat16
HD = 64
SCALE = HD**-0.5
NEG = -1e30
AXES = ("xh", "co", "y", "xl", "z")
CTX = ("y", "xl", "z")
YZ = ("y", "z")
X = ("xh", "xl")
SWAP = [(0, 1), (1, 0)]

PIECE = 72
ORDER = np.full((16, PIECE), -1, np.int32)
for _n in range(16):
    for _xl in range(2):
        _c = (_n // 4) * 8 + _xl * 4 + _n % 4
        ORDER[_n, _xl * 34 : _xl * 34 + 34] = _c * 34 + np.arange(34)
ORDER = ORDER.reshape(-1)
DP = 16 * PIECE


def ring(n, s):
    return [(i, (i + s) % n) for i in range(n)]


def swap(v):
    return lax.ppermute(v, "co", SWAP)


def nt(a, b):
    return lax.dot_general(a, b, (((1,), (1,)), ((), ())), preferred_element_type=F32)


def nn(a, b):
    return lax.dot_general(a, b, (((1,), (0,)), ((), ())), preferred_element_type=F32)


def tn(a, b):
    return lax.dot_general(a, b, (((0,), (0,)), ((), ())), preferred_element_type=F32)


def heads(v):
    return jnp.transpose(v.reshape(2, 64, 17, 64), (0, 2, 1, 3))


def every(v):
    return jnp.broadcast_to(v[:, 16:], (2, 16, 64, 64))


def pairs_of(*parts):
    rows = [jnp.concatenate(pair, axis=3) for pair in parts]
    return jnp.concatenate(rows, axis=2).reshape(32, 64 * len(parts), 128)


def merge(first, last):
    whole = jnp.concatenate([first, last[:, None]], axis=1)
    return jnp.transpose(whole, (0, 2, 1, 3)).reshape(128, 1088)


def take(v, i):
    return lax.dynamic_index_in_dim(v, i, 0, keepdims=False)


def tile_attend(q, k, v, limit, at):
    s = jnp.where(at[:, None] <= limit[None, :], nt(k, q) * SCALE, NEG)
    top = jnp.max(s, axis=0, keepdims=True)
    e = jnp.exp(s - top)
    total = jnp.sum(e, axis=0, keepdims=True)
    out = tn(v, e.astype(BF16)) / total
    return out, top + jnp.log(total)


def tile_back(q, k, v, limit, at, g, out, lse):
    s = jnp.where(at[:, None] <= limit[None, :], nt(k, q) * SCALE, NEG)
    e = jnp.exp(s - lse)
    delta = jnp.sum(g.astype(F32).T * out, axis=0, keepdims=True)
    ds = (e * (nt(v, g) - delta)).astype(BF16)
    return tn(ds, k) * SCALE, nn(ds, q) * SCALE, nn(e.astype(BF16), g)


def rowwise(v):
    return with_layout_constraint(v, Layout(major_to_minor=(0, 1)))


def standardize(values):
    center = values - jnp.mean(values, axis=-1, keepdims=True)
    spread = jnp.mean(center * center, axis=-1, keepdims=True)
    inverse = lax.rsqrt(spread + 1e-05)
    return (center * inverse, inverse)


def norm_back(grad_result, hat, inverse, gain):
    scaled = grad_result * gain
    first = jnp.mean(scaled, axis=-1, keepdims=True)
    second = jnp.mean(scaled * hat, axis=-1, keepdims=True)
    grad_input = inverse * (scaled - first - hat * second)
    return (grad_input, jnp.sum(grad_result * hat, axis=0), jnp.sum(grad_result, axis=0))


def order_matrix():
    order = jnp.asarray(ORDER)
    return (jnp.arange(16 * 68)[:, None] == order[None, :]).astype(BF16)


def to_order(v):
    return nn(v, order_matrix()).astype(BF16)


def from_order(v):
    return nt(v, order_matrix())


def from_order_wide(v):
    high = lax.reduce_precision(v, 8, 7)
    return from_order(high.astype(BF16)) + from_order((v - high).astype(BF16))


def gather_ring(piece, axis, at):
    out = jnp.zeros((4,) + piece.shape, piece.dtype)
    out = lax.dynamic_update_index_in_dim(out, piece, at, 0)
    for s in (1, 3, 2):
        got = lax.ppermute(piece, axis, ring(4, s))
        out = lax.dynamic_update_index_in_dim(out, got, (at + 4 - s) % 4, 0)
    return out


def sum_ring(pieces, axis, at, dim=0):
    total = lax.dynamic_index_in_dim(pieces, at, dim, keepdims=False).astype(F32)
    for s in (1, 3, 2):
        part = lax.dynamic_index_in_dim(pieces, (at + s) % 4, dim, keepdims=False)
        total = total + lax.ppermute(part, axis, ring(4, s)).astype(F32)
    return total


def rows_of_x(four):
    top = jnp.concatenate([four[0], four[2]], axis=1)
    low = jnp.concatenate([four[1], four[3]], axis=1)
    return jnp.concatenate([top, low, jnp.zeros((4, top.shape[1]), top.dtype)], axis=0)


def x_of_rows(rows):
    n = rows.shape[1] // 2
    return jnp.stack([rows[:34, :n], rows[34:68, :n], rows[:34, n:], rows[34:68, n:]])


def body(
    tokens,
    cotangent,
    lengths,
    block_order,
    ln1_gain,
    ln1_bias,
    w_qkv,
    q_bias,
    v_bias,
    w_out,
    out_bias,
    ln2_gain,
    ln2_bias,
    w_fc,
    fc_bias,
    w_proj,
    proj_bias,
):
    d = 1088
    xh, co, y, xl, z = (lax.axis_index(a) for a in AXES)
    ctx = y * 8 + xl * 4 + z
    x = xh * 2 + xl
    even = co == 0

    def both(own, other):
        return jnp.where(even, own, other), jnp.where(even, other, own)

    qkv_piece = rows_of_x(gather_ring(w_qkv, X, x))
    vectors = jnp.concatenate(
        [ln1_gain, ln1_bias, q_bias, v_bias, out_bias, ln2_gain, ln2_bias, proj_bias, fc_bias]
    ).astype(F32)
    vectors, qkv_piece = lax.optimization_barrier((vectors, qkv_piece))
    vectors = lax.all_to_all(
        jnp.broadcast_to(vectors[None], (32, 408)), CTX, split_axis=0, concat_axis=0, tiled=True
    )
    qkv = lax.all_gather(qkv_piece, YZ, axis=0, tiled=True)
    w_fc, w_out, w_proj, vectors = lax.optimization_barrier((w_fc, w_out, w_proj, vectors))
    fc_keep, fc_half = both(w_fc[:, :544], w_fc[:, 544:])
    fc_own = jnp.concatenate(both(fc_keep, swap(fc_half)), axis=1)
    proj_own = lax.ppermute(w_proj, ("co", "xl"), [(0, 0), (1, 2), (2, 1), (3, 3)])
    four = gather_ring(jnp.concatenate([w_out, fc_own], axis=1), X, x)
    out_piece = rows_of_x(four[:, :, :272])
    none = jnp.zeros((PIECE, 272), BF16)
    o0, o1 = both(out_piece[:, :272], none)
    o2, o3 = both(out_piece[:, 272:], none)
    fc_piece = jnp.concatenate([rows_of_x(four[:, :, 272:]), o0, o1, o2, o3], axis=1)
    four = gather_ring(proj_own, X, x)
    proj_piece = jnp.concatenate([four[0], four[1], four[2], four[3]], axis=1)
    fc_piece, proj_piece, qkv = lax.optimization_barrier((fc_piece, proj_piece, qkv))
    fc_out = lax.all_gather(fc_piece, YZ, axis=0, tiled=True)
    proj = lax.all_gather(proj_piece, YZ, axis=0, tiled=True)
    fc = fc_out[:, :2176]
    out_w = fc_out[:, 2176:]

    gain_one, bias_one, query_bias, value_bias, branch_bias, gain_two, bias_two, final_bias = (
        vectors[:, 34 * i : 34 * i + 34].reshape(1, d) for i in range(8)
    )
    hidden_bias = vectors[:, 272:].reshape(4, 2, 544)
    hidden_bias = jnp.where(even, hidden_bias[:, 0], hidden_bias[:, 1]).reshape(1, 2176)

    pair = lax.dynamic_index_in_dim(block_order, ctx, 0, keepdims=False)
    keep = (co + pair) % 2
    sent = jnp.concatenate([tokens, cotangent], axis=0)
    low = keep == 0
    kept = jnp.where(low, sent[:, :64], sent[:, 64:])
    sent = jnp.where(low, sent[:, 64:], sent[:, :64])
    slots = jnp.stack(both(kept, swap(sent)), axis=1).reshape(2, 128, d)
    length = jnp.concatenate(both(lengths, swap(lengths)))
    block = jnp.where(keep == 0, pair, 63 - pair)
    at = block * 64 + jnp.arange(64, dtype=jnp.int32)
    valid = (at[None, :] < length[:, None]).reshape(128, 1)
    mask = valid.astype(F32)

    blocks = 2 * jnp.arange(32, dtype=jnp.int32)[None, :] + jnp.arange(2, dtype=jnp.int32)[:, None]
    pairs = jnp.where(blocks < 32, blocks, 63 - blocks)
    match = pairs[:, :, None] == block_order[None, None, :]
    found = jnp.sum(jnp.where(match, jnp.arange(32, dtype=jnp.int32), 0), axis=2).astype(jnp.int32)
    own = jnp.where(even, found[0], found[1])
    oth = jnp.where(even, found[1], found[0])
    index = (block - co) // 2
    info = jnp.stack(
        [co, ctx % 16, jnp.where(index < 16, index, 31 - index), jnp.where(ctx < 16, length[0], length[1])]
    ).astype(jnp.int32)

    tokens_f = slots[0].astype(F32)
    first_hat, first_inverse = standardize(tokens_f)
    normed = to_order((first_hat * gain_one + bias_one).astype(BF16))
    normed = jnp.concatenate([normed, swap(normed)], axis=0)
    bias = jnp.concatenate([query_bias, jnp.zeros((1, d), F32), value_bias], axis=1)
    bias_a = jnp.where(even, bias[:, :816], bias[:, 816:1632])
    bias_b = jnp.where(even, bias[:, 1632:2448], bias[:, 2448:])
    projected = (nn(normed, qkv) + jnp.concatenate([bias_a, bias_b], axis=1)).astype(BF16)
    mine, theirs = projected[:128], swap(projected[128:])
    f0, f1 = both(mine[:, :816], theirs[:, :816])
    f2, f3 = both(mine[:, 816:], theirs[:, 816:])
    whole = jnp.concatenate([f0, f1, f2, f3], axis=1)
    q, k, v = (heads(whole[:, i * d : i * d + d]) for i in range(3))
    first, last = slice(0, 16), slice(16, 17)
    sent = pairs_of((q[:, first], every(q)), (k[:, first], v[:, first]), (every(v), every(k)))
    xs = lax.all_to_all(sent, CTX, split_axis=0, concat_axis=0, tiled=True)
    xo = swap(xs[:, 64:])
    turn = info[1]
    xs, xo = xs[own], xo[oth]
    inner = jnp.arange(64, dtype=jnp.int32)
    at_q = ((2 * jnp.arange(32, dtype=jnp.int32) + co)[:, None] * 64 + inner).reshape(2048)
    at_o = ((2 * jnp.arange(32, dtype=jnp.int32) + 1 - co)[:, None] * 64 + inner).reshape(2048)
    q_all = xs[:, :64, :64].reshape(2048, 64)
    pair_q = jnp.concatenate([take(xs, turn)[:64, 64:], take(xs, 31 - turn)[:64, 64:]], axis=0)
    k_own, v_own = xs[:, 64:128, :64].reshape(2048, 64), xs[:, 64:128, 64:].reshape(2048, 64)
    k_oth, v_oth = xo[:, :64, :64].reshape(2048, 64), xo[:, :64, 64:].reshape(2048, 64)
    v_16 = jnp.concatenate([xs[:, 128:, :64].reshape(2048, 64), xo[:, 64:, :64].reshape(2048, 64)], axis=0)
    k_16 = jnp.concatenate([xs[:, 128:, 64:].reshape(2048, 64), xo[:, 64:, 64:].reshape(2048, 64)], axis=0)
    bound = info[3] - 1
    at_all = jnp.concatenate([at_q, at_o])
    at_pair = jnp.concatenate([take(at_q.reshape(32, 64), turn), take(at_q.reshape(32, 64), 31 - turn)])
    tiles = []
    for j in range(4):
        r, n = slice(512 * j, 512 * j + 512), slice(0, 512 * j + 512)
        keys = jnp.concatenate([k_own[n], k_oth[n]], axis=0)
        values = jnp.concatenate([v_own[n], v_oth[n]], axis=0)
        at = jnp.concatenate([at_q[n], at_o[n]])
        limit = jnp.minimum(at_q[r], bound)
        tiles.append((r, n, keys, values, limit, at, q_all[r]))
    outs = [tile_attend(q, keys, values, limit, at) for r, n, keys, values, limit, at, q in tiles]
    pair_limit = jnp.minimum(at_pair, bound)
    out_16, lse_16 = tile_attend(pair_q, k_16, v_16, pair_limit, at_all)
    inverse = jnp.sum(jnp.where(own[None, :] == jnp.arange(32)[:, None], jnp.arange(32), 0), axis=1)
    is_turn = jnp.arange(32)[:, None, None]
    low_16 = out_16.T.reshape(2, 64, 64)
    wide = jnp.where(is_turn == turn, low_16[0], jnp.where(is_turn == 31 - turn, low_16[1], 0.0))
    low_all = jnp.concatenate([o.T for o, _ in outs], axis=0).reshape(32, 64, 64)
    o_sent = jnp.concatenate([wide, low_all], axis=2).astype(BF16)[inverse]
    o_got = lax.all_to_all(o_sent, CTX, split_axis=0, concat_axis=0, tiled=True)
    o_got = o_got.reshape(2, 16, 64, 128)
    home_turn = info[2]

    def turned(v):
        return lax.dynamic_index_in_dim(v, home_turn, 1, keepdims=False)

    attended = to_order(merge(o_got[..., 64:], turned(o_got[..., :64])))
    attended = jnp.concatenate([attended, swap(attended)], axis=0)
    branch = nn(attended, out_w)
    middle = tokens_f + (branch[:128] + swap(branch[128:])) + branch_bias
    second_hat, second_inverse = standardize(middle)
    second = to_order((second_hat * gain_two + bias_two).astype(BF16))
    second = jnp.concatenate([second, swap(second)], axis=0)
    hidden = nn(second, fc) + hidden_bias
    active, gelu_pull = jax.vjp(lambda h: jax.nn.gelu(h, approximate=True), hidden)
    active = lax.reduce_precision(active, 8, 7).astype(BF16)
    final = nn(active, proj)
    final = final[:128] + swap(final[128:]) + final_bias
    layer_out = (mask * (middle + final)).astype(BF16)

    grad_out_low = jnp.where(valid, slots[1], BF16(0))
    grad_out = grad_out_low.astype(F32)
    grad_out_two = jnp.concatenate([grad_out_low, swap(grad_out_low)], axis=0)
    (grad_hidden,) = gelu_pull(nt(grad_out_two, proj))
    grad_hidden = lax.reduce_precision(grad_hidden, 8, 7)
    hidden_sum = jnp.sum(grad_hidden, axis=0)
    grad_hidden = grad_hidden.astype(BF16)
    grad_second = nt(grad_hidden, fc)
    grad_second = from_order_wide(grad_second[:128] + swap(grad_second[128:]))
    grad_mid, g_ln2_gain, g_ln2_bias = norm_back(grad_second, second_hat, second_inverse, gain_two)
    grad_middle = grad_out + grad_mid
    grad_branch = lax.reduce_precision(grad_middle, 8, 7)
    branch_sum = jnp.sum(grad_branch, axis=0)
    grad_branch = grad_branch.astype(BF16)
    whole_branch = both_branch = jnp.concatenate([grad_branch, swap(grad_branch)], axis=0)
    both_branch = jnp.concatenate(
        [
            jnp.where(even, both_branch[:, :272], both_branch[:, 272:544]),
            jnp.where(even, both_branch[:, 544:816], both_branch[:, 816:]),
        ],
        axis=1,
    )
    grad_attn = nt(whole_branch, out_w)
    grad_attn = (grad_attn[:128] + swap(grad_attn[128:])).astype(BF16)
    grad_attn = from_order(grad_attn).astype(BF16)
    g = heads(grad_attn)
    sent = pairs_of((every(g), g[:, first]))
    sent, active, grad_out_two, second, grad_hidden, attended, both_branch = lax.optimization_barrier(
        (sent, active, grad_out_two, second, grad_hidden, attended, both_branch)
    )
    ga = lax.all_to_all(sent, CTX, split_axis=0, concat_axis=0, tiled=True)
    g_proj = rowwise(tn(active, grad_out_two).astype(BF16)).reshape(16, 136, d)
    g_fc = [rowwise(tn(second, grad_hidden[:, i * d : i * d + d]).astype(BF16)).reshape(16, PIECE, d) for i in range(2)]
    g_out = jnp.pad(rowwise(tn(attended, both_branch).astype(BF16)).reshape(16, PIECE, 544), ((0, 0), (0, 0), (0, 544)))
    packed = jnp.concatenate(g_fc + [g_out, g_proj], axis=1)
    packed = lax.psum_scatter(packed.reshape(16 * 352, d), YZ, scatter_dimension=0, tiled=True)
    packed = lax.optimization_barrier(packed)
    ga = ga[own]
    g_all = ga[:, :, 64:].reshape(2048, 64)
    pair_g = jnp.concatenate([take(ga, turn)[:, :64], take(ga, 31 - turn)[:, :64]], axis=0)
    dqs = []
    dk = [jnp.zeros((2048, 64), F32), jnp.zeros((2048, 64), F32)]
    dv = [jnp.zeros((2048, 64), F32), jnp.zeros((2048, 64), F32)]
    for (r, n, keys, values, limit, at, q), (out, lse) in zip(tiles, outs):
        dq, dk_part, dv_part = tile_back(q, keys, values, limit, at, g_all[r], out, lse)
        dqs.append(dq)
        rows = n.stop
        for i in range(2):
            grow = ((0, 2048 - rows), (0, 0))
            dk[i] = dk[i] + jnp.pad(dk_part[i * rows : i * rows + rows], grow)
            dv[i] = dv[i] + jnp.pad(dv_part[i * rows : i * rows + rows], grow)
    dq_16, dk_16, dv_16 = tile_back(pair_q, k_16, v_16, pair_limit, at_all, pair_g, out_16, lse_16)
    dq_16 = dq_16.reshape(2, 64, 64)
    wide = jnp.where(is_turn == turn, dq_16[0], jnp.where(is_turn == 31 - turn, dq_16[1], 0.0))
    dq = jnp.concatenate([jnp.concatenate(dqs, axis=0).reshape(32, 64, 64), wide], axis=2).astype(BF16)
    mine = jnp.concatenate([dk[0], dv[0], dv_16[:2048], dk_16[:2048]], axis=1)
    theirs = jnp.concatenate([dk[1], dv[1], dv_16[2048:], dk_16[2048:]], axis=1).astype(BF16)
    total = (mine + swap(theirs).astype(F32)).astype(BF16).reshape(32, 64, 256)
    sent = jnp.concatenate([dq, total[:, :, :128], total[:, :, 128:]], axis=1)[inverse]
    got = lax.all_to_all(sent, CTX, split_axis=0, concat_axis=0, tiled=True)
    got = got.reshape(2, 16, 192, 128)
    last = jnp.sum(got[:, :, 128:].astype(F32), axis=1).astype(BF16)
    grad_projected = jnp.concatenate(
        [
            merge(got[:, :, :64, :64], turned(got[:, :, :64, 64:])),
            merge(got[:, :, 64:128, :64], last[:, :, 64:]),
            merge(got[:, :, 64:128, 64:], last[:, :, :64]),
        ],
        axis=1,
    )
    columns_sum = jnp.sum(grad_projected.astype(F32), axis=0)
    f0, f1 = both(grad_projected[:, :816], grad_projected[:, 816:1632])
    f2, f3 = both(grad_projected[:, 1632:2448], grad_projected[:, 2448:])
    part_a = jnp.concatenate([f0, swap(f1)], axis=0)
    part_b = jnp.concatenate([f2, swap(f3)], axis=0)
    fc_rows = jnp.concatenate([packed[:PIECE], packed[PIECE : 2 * PIECE]], axis=1)
    out_rows = packed[2 * PIECE : 3 * PIECE, :544]
    proj_rows = packed[3 * PIECE :]
    proj_x = jnp.stack([proj_rows[:, i * 272 : i * 272 + 272] for i in range(4)])
    proj_sum = sum_ring(proj_x, X, x)
    proj_sum = lax.ppermute(proj_sum, ("co", "xl"), [(0, 0), (1, 2), (2, 1), (3, 3)])
    fc_x = jnp.concatenate([x_of_rows(fc_rows), x_of_rows(out_rows)], axis=2)
    fc_sum = sum_ring(fc_x, X, x)
    out_sum = fc_sum[:, 1088:]
    h0, h1 = both(fc_sum[:, :544], fc_sum[:, 544:1088])
    h0, h1 = both(h0, swap(h1))
    fc_sum = jnp.concatenate([h0, h1], axis=1)

    grad_normed = nt(jnp.concatenate([part_a, part_b], axis=1), qkv)
    grad_normed = from_order_wide(grad_normed[:128] + swap(grad_normed[128:]))
    grad_in, g_ln1_gain, g_ln1_bias = norm_back(grad_normed, first_hat, first_inverse, gain_one)
    grad_tokens = (grad_middle + grad_in).astype(BF16)

    g_hidden_bias = hidden_sum.reshape(4, 1, 544)
    zero = jnp.zeros_like(g_hidden_bias)
    g_hidden_bias = jnp.concatenate(both(g_hidden_bias, zero), axis=1).reshape(32, 136)
    sums = [
        g_ln1_gain,
        g_ln1_bias,
        columns_sum[:d],
        columns_sum[2 * d :],
        branch_sum,
        g_ln2_gain,
        g_ln2_bias,
        jnp.sum(grad_out, axis=0),
    ]
    sums = jnp.concatenate([v.reshape(32, 34) for v in sums] + [g_hidden_bias], axis=1)
    sums = sums + swap(sums)
    g_a = rowwise(tn(normed, part_a).astype(BF16)).reshape(16, PIECE, 816)
    g_b = rowwise(tn(normed, part_b).astype(BF16)).reshape(16, PIECE, 816)
    riders = jnp.transpose(sums.astype(BF16).reshape(4, 2, 4, 408), (0, 2, 1, 3)).reshape(16, 2, 408)
    g_a = lax.dynamic_update_slice(g_a, riders, (0, 68, 0)).reshape(4, 4 * PIECE, 816)
    g_b = lax.dynamic_update_slice(g_b, riders, (0, 68, 0)).reshape(4, 4, PIECE, 816)
    fc_sum, out_sum, proj_sum, g_a, g_b = lax.optimization_barrier((fc_sum, out_sum, proj_sum, g_a, g_b))
    g_a = sum_ring(g_a, "y", y).astype(BF16)
    g_b = sum_ring(g_b, "z", z, 1).astype(BF16)
    g_a = sum_ring(g_a.reshape(4, PIECE, 816), "z", z).astype(BF16)
    g_b = sum_ring(g_b, "y", y).astype(BF16)
    parts = [(g, r) for g in (g_a, g_b) for r in range(2)]
    g_qkv = jnp.stack([jnp.concatenate([g[34 * r : 34 * r + 34], g[68 + r : 69 + r]], axis=0) for g, r in parts])
    qkv_sum = sum_ring(g_qkv, X, x)
    sums = qkv_sum[34, :408]
    sums = jnp.where(xh == 0, sums, lax.ppermute(sums, "xh", SWAP))
    qkv_sum = qkv_sum[:34]

    results = jnp.stack([layer_out, grad_tokens])
    first, last = results[:, :64], results[:, 64:]
    home = jnp.where(even, first, last)
    away = swap(jnp.where(even, last, first))
    placed = jnp.concatenate([jnp.where(low, home, away), jnp.where(low, away, home)], axis=1)

    v = [sums[34 * i : 34 * i + 34] for i in range(8)]
    return (
        placed[0][None],
        placed[1][None],
        v[0],
        v[1],
        qkv_sum,
        v[2],
        v[3],
        out_sum,
        v[4],
        v[5],
        v[6],
        fc_sum,
        sums[272:],
        proj_sum,
        v[7],
    )


def solution(mesh):
    grid = Mesh(mesh.devices.reshape(2, 2, 4, 2, 4), AXES)
    f = ("xh", "co")
    rows = P(f, CTX, None)
    matrix = P(CTX, f)
    vector = P(CTX)
    ins = (rows, rows, P(f), P(), vector, vector, matrix, vector, vector, matrix)
    ins = ins + (vector, vector, vector, matrix, vector, matrix, vector)
    outs = (rows, rows, vector, vector, matrix, vector, vector, matrix, vector, vector, vector)
    outs = outs + (matrix, vector, matrix, vector)
    return jax.shard_map(body, mesh=grid, in_specs=ins, out_specs=outs, check_vma=False)
```
